32 devices in a mesh: groups: 2 (over y), tensor: 4 (over z), bank: 2 (over x), pipe: 2 (over core).
Axes of the slice: x: 2, y: 2, z: 4, core: 2. Of those that a mesh axis runs over, the one named last changes fastest.
Arguments:
- x_in: bfloat16 [4096, 5120], P(('groups', 'bank', 'pipe'), 'tensor'), parts along dimension 0, may hold values from -6 to 6
- grad_out: bfloat16 [4096, 5120], P(('groups', 'bank', 'pipe'), 'tensor'), parts along dimension 0, may hold values from -6 to 6
- gate_pre: bfloat16 [4096, 17408], P(('groups', 'bank', 'pipe'), 'tensor'), parts along dimension 0, may hold values from -6 to 6
- up_pre: bfloat16 [4096, 17408], P(('groups', 'bank', 'pipe'), 'tensor'), parts along dimension 0, may hold values from -6 to 6
- w_down: bfloat16 [17408, 5120], P('tensor', 'pipe'), may hold values from -0.046875 to 0.046875
- proj_in: bfloat16 [5120, 64], P('tensor'), may hold values from -0.078125 to 0.078125
- proj_ff: bfloat16 [17408, 64], P('tensor'), may hold values from -0.046875 to 0.046875
- resp_mask: int32 [4096], P(('groups', 'bank', 'pipe')), parts along dimension 0, may hold values 0 or 1
- doc_lengths: int32 [16], P('groups'), parts along dimension 0, may hold values from 1 to 1024, 2048 in all
- owner: int32 [16], P('groups'), parts along dimension 0, may hold values from 0 to 1, as said below
- bank_grads: bfloat16 [2, 256, 12288], P('bank', 'pipe', 'tensor'), may hold values from -0.0034179688 to 0.0034179688
Outputs:
- scores: float32 [16, 256], P('groups', 'pipe'), parts along dimension 0
The draws below stay inside these ranges and needn't reach their ends.
There are 2 independent parts, one for each index of `groups`. The reference program is written for one: setup_inputs(seed, part) draws one part's arguments, and reference() takes and returns one part's arrays. A program takes and returns all parts, laid end to end along the dimension named above; an argument that names none is the same for every part. Nothing has to cross between parts.
Inputs may be any that keep to these rules, and one draw needn't show every extreme that they name: Each owner is named by exactly 4 examples. `doc_lengths`: the lengths sum to 2048.
All inputs are finite; a program needn't handle non-finite values. No bound on the sum of `resp_mask` on one device may be relied on, other than what follows from the above.
Results may differ from the reference program's by a relative error of at most 0.0029.
Values may be sent and summed in bfloat16 or wider, within the bound.
A program may use at most 128 MiB of HBM per device.

```python
import math
import jax
import jax.numpy as jnp
import numpy as np
from jax import lax

D = 5120
FF = 17408
R = 64
KRON = 12288
VAL_OWN = 256
TOKENS = 2048
NEX = 8
MOST = 1024
N_BANK = 2


def draw_owner(key, part):
    key = jax.random.fold_in(key, 7)
    shuffled = jax.random.permutation(key, NEX)
    base = (shuffled % N_BANK).astype(jnp.int32)
    target = jnp.asarray(part, jnp.int32) % N_BANK
    return ((base - base[0] + target) % N_BANK).astype(jnp.int32)


def place_ends(array, key, smallest, largest):
    longest = array.shape.index(max(array.shape))
    spots = []
    for shift in (0, 1):
        where = [jax.random.randint(jax.random.fold_in(key, axis), (), 0, length) for axis, length in enumerate(array.shape)]
        where[longest] = (where[longest] + shift) % array.shape[longest]
        spots.append(tuple(where))
    return array.at[spots[0]].set(smallest).at[spots[1]].set(largest)


def block_levels(stream_key, dims, shards, smallest, high):
    factor_of, own = 1.0, jax.random.fold_in(stream_key, 6)
    for axis_at, shards_of in shards:
        heights = jnp.exp(jax.random.uniform(jax.random.fold_in(own, axis_at), (shards_of,), jnp.float32, smallest / len(shards), high / len(shards)))
        factor_of = factor_of * jnp.repeat(heights, dims[axis_at] // shards_of).reshape([-1 if axis == axis_at else 1 for axis in range(len(dims))])
    return factor_of


def profile(count, total, reach, skew):
    weights = [(1 << 20) // math.isqrt(standing ** skew) + 1 for standing in range(2, count + 1)]
    spare, holding = total - reach - (count - 1), [1] * (count - 1)
    while spare > 0:
        free = [i for i in range(count - 1) if holding[i] < reach]
        pool, remaining = sum([weights[i] for i in free]), spare
        for i in free:
            extra = min(reach - holding[i], max(1, remaining * weights[i] // pool), spare)
            holding[i] = holding[i] + extra
            spare = spare - extra
    return np.array([reach] + holding)


def ragged(rng, amount, total, most, lean):
    if amount == 2:
        one = jax.random.randint(rng, (), max(1, total - most), min(most, total - 1) + 1)
        return jnp.stack([one, total - one])
    lengths = jnp.asarray(profile(amount, total, most, lean), jnp.int32)
    pairs = (amount - 1) // 2
    giver, sink = lengths[1:1 + 2 * pairs:2], lengths[2:2 + 2 * pairs:2]
    margin = jnp.minimum(giver - 1, most - sink)
    shifted = jax.random.randint(jax.random.fold_in(rng, 1), (pairs,), 0, 1 << 20) % (margin + 1)
    lengths = lengths.at[1:1 + 2 * pairs:2].set(giver - shifted).at[2:2 + 2 * pairs:2].set(sink + shifted)
    return lengths[jax.random.permutation(jax.random.fold_in(rng, 2), amount)]


def scatter_about(key, dims, width, reach, pieces=(), kind=jnp.bfloat16):
    factor_of = block_levels(key, dims, pieces, -0.22, 0.18) if pieces else 1.0
    entries = jax.random.normal(key, dims, jnp.float32) * width * factor_of
    return jnp.minimum(jnp.maximum(entries, -reach), reach).astype(kind)


def setup_inputs(seed: int = 0, part: int = 0) -> dict:
    keys = jax.random.split(jax.random.key(seed), 12)
    part_splits = jax.random.split(jax.random.fold_in(keys[11], part), 12)
    return {
        "x_in": scatter_about(part_splits[0], (TOKENS, D), 1.0, 6.0, ((0, 4), (1, 4))),
        "grad_out": scatter_about(part_splits[1], (TOKENS, D), 1.0, 6.0, ((0, 4), (1, 4))),
        "gate_pre": scatter_about(part_splits[2], (TOKENS, FF), 1.0, 6.0, ((0, 4), (1, 4))),
        "up_pre": scatter_about(part_splits[3], (TOKENS, FF), 1.0, 6.0, ((0, 4), (1, 4))),
        "w_down": scatter_about(keys[4], (FF, D), FF ** -0.5, 0.046875, ((0, 4), (1, 2))),
        "proj_in": scatter_about(keys[5], (D, R), D ** -0.5, 0.078125, ((0, 4),)),
        "proj_ff": scatter_about(keys[6], (FF, R), FF ** -0.5, 0.046875, ((0, 4),)),
        "resp_mask": place_ends((jax.random.randint(part_splits[7], (TOKENS,), 0, 2) < 1).astype(jnp.int32), jax.random.fold_in(part_splits[7], 1), 0, 1),
        "doc_lengths": ragged(part_splits[8], NEX, TOKENS, MOST, 1).astype(jnp.int32),
        "owner": draw_owner(jax.random.fold_in(jax.random.fold_in(keys[11], part), 71), part),
        "bank_grads": scatter_about(keys[10], (N_BANK, VAL_OWN, KRON), (KRON * MOST // 4) ** -0.5, 0.0034179688, ((0, 2), (1, 2), (2, 4))),
    }


def module_grad(member, left_proj, right_proj):
    return jnp.einsum('te,ti,tj->eij', member, left_proj, right_proj, precision=lax.Precision.HIGHEST)

def reference(x_in, grad_out, gate_pre, up_pre, w_down, proj_in, proj_ff, resp_mask, doc_lengths, owner, bank_grads):
    hidden_grad = jnp.dot(grad_out, w_down.T, preferred_element_type=jnp.float32)
    gate_val = gate_pre.astype(jnp.float32)
    up_val = up_pre.astype(jnp.float32)
    sigmoid_gate = jax.nn.sigmoid(gate_val)
    activated = gate_val * sigmoid_gate
    slope = sigmoid_gate * (1.0 + gate_val * (1.0 - sigmoid_gate))
    hidden = (activated * up_val).astype(jnp.bfloat16)
    up_grad = (hidden_grad * activated).astype(jnp.bfloat16)
    gate_grad = (hidden_grad * up_val * slope).astype(jnp.bfloat16)
    a_down = jnp.dot(hidden, proj_ff, preferred_element_type=jnp.float32)
    b_up = jnp.dot(up_grad, proj_ff, preferred_element_type=jnp.float32)
    b_gate = jnp.dot(gate_grad, proj_ff, preferred_element_type=jnp.float32)
    a_in = jnp.dot(x_in, proj_in, preferred_element_type=jnp.float32)
    b_down = jnp.dot(grad_out, proj_in, preferred_element_type=jnp.float32)
    doc_ends = jnp.cumsum(doc_lengths).astype(jnp.int32)
    starts = (doc_ends - doc_lengths).astype(jnp.int32)
    positions = jnp.arange(TOKENS, dtype=jnp.int32)
    inside = (positions[:, None] >= starts[None, :]) & (positions[:, None] < doc_ends[None, :])
    member = inside.astype(jnp.float32) * resp_mask.astype(jnp.float32)[:, None]
    grads = jnp.stack([module_grad(member, a_down, b_down), module_grad(member, a_in, b_up), module_grad(member, a_in, b_gate)], axis=1)
    example_grads = grads.reshape(NEX, KRON)
    own_bank = bank_grads.astype(jnp.float32)[owner]
    return jnp.einsum('ek,evk->ev', example_grads, own_bank, precision=lax.Precision.HIGHEST)
```

```python
import functools
import jax
import jax.numpy as jnp
import numpy as np
from jax import lax
from jax.sharding import PartitionSpec as P
from jax.experimental import pallas as pl
from jax.experimental.pallas import tpu as pltpu

MESH = pl.DeviceIdType.MESH
VMEM = pl.BlockSpec(memory_space=pltpu.VMEM)
CAP = 320
PIECES = 4
LIMIT = 56 * 1024 * 1024
LAST = (((1,), (1,)), ((), ()))


def body(
    x_in,
    grad_out,
    gate_pre,
    up_pre,
    w_down,
    proj_in,
    proj_ff,
    resp_mask,
    doc_lengths,
    owner,
    bank_grads,
):
    rows_here = x_in.shape[0]
    proj_rank = proj_in.shape[1]
    contract_last = (((1,), (1,)), ((), ()))
    full_rows = lax.all_gather(grad_out, "tensor", axis=1, tiled=True)
    paired = lax.all_to_all(full_rows, "pipe", split_axis=1, concat_axis=0, tiled=True)
    hidden_grad = lax.psum_scatter(
        lax.dot_general(paired, w_down, contract_last, preferred_element_type=jnp.float32),
        "pipe",
        scatter_dimension=0,
        tiled=True,
    )
    gate_val = gate_pre.astype(jnp.float32)
    up_val = up_pre.astype(jnp.float32)
    sigmoid_gate = jax.nn.sigmoid(gate_val)
    activated = gate_val * sigmoid_gate
    slope = sigmoid_gate * (1.0 + gate_val * (1.0 - sigmoid_gate))
    hidden = (activated * up_val).astype(jnp.bfloat16)
    up_grad = (hidden_grad * activated).astype(jnp.bfloat16)
    gate_grad = (hidden_grad * up_val * slope).astype(jnp.bfloat16)
    wide_side = jnp.stack([hidden, up_grad, gate_grad])
    wide_proj = jnp.einsum("stf,fr->srt", wide_side, proj_ff, preferred_element_type=jnp.float32)
    narrow_side = jnp.stack([x_in, grad_out])
    narrow_proj = jnp.einsum(
        "std,dr->srt", narrow_side, proj_in, preferred_element_type=jnp.float32
    )
    partials = jnp.concatenate([wide_proj, narrow_proj], axis=0)
    projected = lax.psum(partials, "tensor")
    stacked = projected.reshape(5 * proj_rank, rows_here)
    kron_part = bank_grads.shape[2]
    square = proj_rank * proj_rank
    module_ids = np.repeat(np.arange(3), square)
    inner_ids = np.arange(3 * square) % square
    left_table = np.array([0, 3, 3])[module_ids] * proj_rank + inner_ids // proj_rank
    right_table = np.array([4, 1, 2])[module_ids] * proj_rank + inner_ids % proj_rank
    first_entry = lax.axis_index("tensor") * kron_part
    left_ids = lax.dynamic_slice_in_dim(jnp.asarray(left_table, jnp.int32), first_entry, kron_part)
    right_ids = lax.dynamic_slice_in_dim(
        jnp.asarray(right_table, jnp.int32), first_entry, kron_part
    )
    products = jnp.take(stacked, left_ids, axis=0) * jnp.take(stacked, right_ids, axis=0)
    offset = lax.axis_index(("bank", "pipe")) * rows_here
    positions = offset + jnp.arange(rows_here, dtype=jnp.int32)
    doc_ends = jnp.cumsum(doc_lengths)
    starts = doc_ends - doc_lengths
    inside = (positions[:, None] >= starts[None, :]) & (positions[:, None] < doc_ends[None, :])
    member = inside.astype(jnp.float32) * resp_mask.astype(jnp.float32)[:, None]
    grad_part = lax.dot_general(
        member,
        products,
        (((0,), (1,)), ((), ())),
        precision=lax.Precision.HIGHEST,
        preferred_element_type=jnp.float32,
    )
    example_grads = lax.psum(grad_part, ("bank", "pipe"))
    own_rows = bank_grads[0].astype(jnp.float32)
    partial_value = lax.dot_general(
        example_grads,
        own_rows,
        contract_last,
        precision=lax.Precision.HIGHEST,
        preferred_element_type=jnp.float32,
    )
    owned = (owner == lax.axis_index("bank")).astype(jnp.float32)[:, None]
    scores = lax.psum(partial_value * owned, ("tensor", "bank"))
    return scores


def params(cid, **more):
    return pltpu.CompilerParams(
        collective_id=cid, has_side_effects=True, vmem_limit_bytes=LIMIT, **more
    )


def greet(devices):
    barrier = pltpu.get_barrier_semaphore()
    for device in devices:
        pl.semaphore_signal(barrier, inc=1, device_id=device, device_id_type=MESH)
    pl.semaphore_wait(barrier, len(devices))


def gather_kernel(nz, half, pick, grad, x_in, proj, buf, narrow, packed, own_sem, fwd_sem, recv_sem):
    z, c = lax.axis_index("tensor"), lax.axis_index("pipe")
    other = 1 - c
    dest, place = z // half, z % half
    rows = packed.shape[0] // PIECES
    barrier = pltpu.get_barrier_semaphore()
    pl.semaphore_signal(barrier, inc=1, device_id={"pipe": other}, device_id_type=MESH)
    for step in (-1, 1):

        @pl.when((z + step >= 0) & (z + step < nz))
        def _():
            for core in range(2):
                pl.semaphore_signal(
                    barrier,
                    inc=1,
                    device_id={"tensor": z + step, "pipe": core},
                    device_id_type=MESH,
                )

    inner = jnp.where((z > 0) & (z < nz - 1), 5, 3)
    packed[...] = jnp.dot(pick[...], grad[...], preferred_element_type=jnp.float32).astype(
        jnp.bfloat16
    )
    pl.semaphore_wait(barrier, inner)

    def piece(q):
        return pl.ds(q * rows, rows)

    def own(way, q):
        device = {"tensor": z + (1, -1, 0)[way], "pipe": dest}
        return pltpu.make_async_remote_copy(
            src_ref=packed.at[piece(q)],
            dst_ref=buf.at[place, c, piece(q)],
            send_sem=own_sem.at[way, q],
            recv_sem=recv_sem.at[place, c, q],
            device_id=device,
            device_id_type=MESH,
        )

    goes = (z < nz - 1, z > 0, dest != c)

    for q in range(PIECES):
        for way in range(3):

            @pl.when(goes[way])
            def _():
                own(way, q).start()

    @pl.when(dest == c)
    def _():
        buf[place, c] = packed[...]

    packed_x = jnp.dot(pick[...], x_in[...], preferred_element_type=jnp.float32).astype(
        jnp.bfloat16
    )
    narrow[:, 0:64] = jnp.dot(packed_x, proj[...], preferred_element_type=jnp.float32)
    narrow[:, 64:128] = jnp.dot(packed[...], proj[...], preferred_element_type=jnp.float32)

    def passed(j, k, q, step):
        return pltpu.make_async_remote_copy(
            src_ref=buf.at[j, k, piece(q)],
            dst_ref=buf.at[j, k, piece(q)],
            send_sem=fwd_sem.at[j, k, q],
            recv_sem=recv_sem.at[j, k, q],
            device_id={"tensor": z + step, "pipe": c},
            device_id_type=MESH,
        )

    def each(do):
        for q in range(PIECES):
            for i in range(half):
                j = c * i + (1 - c) * (half - 1 - i)
                source = c * half + j
                for k in range(2):
                    do(j, k, q, source)

    def receive(j, k, q, source):
        @pl.when((source != z) | (k != c))
        def _():
            passed(j, k, q, 0).wait_recv()

        @pl.when((source < z) & (z < nz - 1))
        def _():
            passed(j, k, q, 1).start()

        @pl.when((source > z) & (z > 0))
        def _():
            passed(j, k, q, -1).start()

    def finish(j, k, q, source):
        @pl.when(((source < z) & (z < nz - 1)) | ((source > z) & (z > 0)))
        def _():
            passed(j, k, q, 0).wait_send()

    each(receive)
    for q in range(PIECES):
        for way in range(3):

            @pl.when(goes[way])
            def _():
                own(way, q).wait_send()

    each(finish)


def hidden_kernel(tiles, half, buf, weight, gate, up, proj, pick, out, mine, sent, got, send_sem, recv_sem):
    i = pl.program_id(0)
    c = lax.axis_index("pipe")
    width = buf.shape[3]

    def copy(t):
        return pltpu.make_async_remote_copy(
            src_ref=sent.at[t],
            dst_ref=got.at[t],
            send_sem=send_sem.at[t],
            recv_sem=recv_sem.at[t],
            device_id={"pipe": 1 - c},
            device_id_type=MESH,
        )

    def part(core):
        total = None
        for j in range(half):
            term = lax.dot_general(
                buf[j, core],
                weight[:, j * width : (j + 1) * width],
                LAST,
                preferred_element_type=jnp.float32,
            )
            total = term if total is None else total + term
        return total

    @pl.when(i == 0)
    def _():
        greet([{"pipe": 1 - c}])
        out[...] = jnp.zeros_like(out)

    @pl.when(i < tiles)
    def _():
        sent[i] = part(1 - c).astype(jnp.bfloat16)
        copy(i).start()
        mine[i % 2] = part(c)

    @pl.when(i > 0)
    def _():
        t = i - 1
        gate_val = jnp.dot(pick[...], gate[...], preferred_element_type=jnp.float32)
        up_val = jnp.dot(pick[...], up[...], preferred_element_type=jnp.float32)
        sig = jax.nn.sigmoid(gate_val)
        act = gate_val * sig
        slope = sig * (1.0 + gate_val * (1.0 - sig))
        table = proj[...]
        out[0] += jnp.dot(
            (act * up_val).astype(jnp.bfloat16), table, preferred_element_type=jnp.float32
        )
        copy(t).wait_recv()
        grad = mine[t % 2] + got[t].astype(jnp.float32)
        out[1] += jnp.dot(
            (grad * act).astype(jnp.bfloat16), table, preferred_element_type=jnp.float32
        )
        out[2] += jnp.dot(
            (grad * up_val * slope).astype(jnp.bfloat16),
            table,
            preferred_element_type=jnp.float32,
        )

    @pl.when(i == tiles)
    def _():
        @pl.loop(0, tiles)
        def _(t):
            copy(t).wait_send()


def tensor_sum_kernel(n, part, out, got, send_sem, recv_sem, send2, recv2):
    me = lax.axis_index("tensor")
    peers = [lax.rem(me + d, n) for d in range(1, n)]
    greet([{"tensor": peer} for peer in peers])

    def first(peer, slot):
        return pltpu.make_async_remote_copy(
            src_ref=part.at[peer],
            dst_ref=got.at[slot],
            send_sem=send_sem.at[peer],
            recv_sem=recv_sem.at[slot],
            device_id={"tensor": peer},
            device_id_type=MESH,
        )

    def second(peer, slot):
        return pltpu.make_async_remote_copy(
            src_ref=out.at[slot],
            dst_ref=out.at[slot],
            send_sem=send2.at[peer],
            recv_sem=recv2.at[slot],
            device_id={"tensor": peer},
            device_id_type=MESH,
        )

    for peer in peers:
        first(peer, me).start()
    got[me] = part[me]
    for peer in peers:
        first(peer, peer).wait_recv()
    total = got[0]
    for k in range(1, n):
        total = total + got[k]
    out[me] = total
    for peer in peers:
        second(peer, me).start()
    for peer in peers:
        second(peer, peer).wait_recv()
    for peer in peers:
        first(peer, me).wait_send()
        second(peer, me).wait_send()


def small_sum_kernel(axes, count_axes, *refs):
    if count_axes:
        part, count, out, counts, got, send_sem, recv_sem, csend, crecv = refs
    else:
        part, out, got, send_sem, recv_sem = refs

    def layout(names):
        sizes = [lax.axis_size(a) for a in names]
        me = lax.axis_index(names[0])
        for name, size in zip(names[1:], sizes[1:]):
            me = me * size + lax.axis_index(name)
        n = int(np.prod(sizes))
        peers = []
        for d in range(1, n):
            flat = lax.rem(me + d, n)
            rest, device = flat, {}
            for name, size in reversed(list(zip(names, sizes))):
                device[name] = lax.rem(rest, size)
                rest = rest // size
            peers.append((flat, device))
        return n, me, peers

    n, me, peers = layout(axes)

    def copy(flat, device, slot):
        return pltpu.make_async_remote_copy(
            src_ref=part,
            dst_ref=got.at[slot],
            send_sem=send_sem.at[flat],
            recv_sem=recv_sem.at[slot],
            device_id=device,
            device_id_type=MESH,
        )

    if count_axes:
        cn, cme, cpeers = layout(count_axes)

        def ccopy(flat, device, slot):
            return pltpu.make_async_remote_copy(
                src_ref=count,
                dst_ref=counts.at[slot],
                send_sem=csend.at[flat],
                recv_sem=crecv.at[slot],
                device_id=device,
                device_id_type=MESH,
            )

        greet([device for _, device in cpeers])
    else:
        greet([device for _, device in peers])
    for flat, device in peers:
        copy(flat, device, me).start()
    if count_axes:
        for flat, device in cpeers:
            ccopy(flat, device, cme).start()
        counts[cme] = count[...]
    got[me] = part[...]
    for flat, device in peers:
        copy(flat, device, flat).wait_recv()
    total = got[0]
    for k in range(1, n):
        total = total + got[k]
    out[...] = total
    for flat, device in peers:
        copy(flat, device, me).wait_send()
    if count_axes:
        for flat, device in cpeers:
            ccopy(flat, device, flat).wait_recv()
        for flat, device in cpeers:
            ccopy(flat, device, cme).wait_send()


def packed_body(
    x_in,
    grad_out,
    gate_pre,
    up_pre,
    w_down,
    proj_in,
    proj_ff,
    resp_mask,
    doc_lengths,
    owner,
    bank_grads,
):
    nz, npipe = lax.axis_size("tensor"), lax.axis_size("pipe")
    half = nz // npipe
    tokens, width = grad_out.shape
    hidden_units = gate_pre.shape[1]
    rank = proj_in.shape[1]
    tile = 256
    tiles = hidden_units // tile
    f32, b16 = jnp.float32, jnp.bfloat16
    dma = pltpu.SemaphoreType.DMA

    order = jnp.cumsum(resp_mask) - 1
    taken = jnp.sum(resp_mask)
    pick = ((order[None, :] == jnp.arange(CAP)[:, None]) & (resp_mask[None, :] > 0)).astype(b16)
    offset = lax.axis_index(("bank", "pipe")) * tokens
    positions = offset + jnp.arange(tokens, dtype=jnp.int32)
    doc_ends = jnp.cumsum(doc_lengths)
    starts = doc_ends - doc_lengths
    inside = (positions[:, None] >= starts[None, :]) & (positions[:, None] < doc_ends[None, :])
    member = jnp.dot(pick, inside.astype(b16), preferred_element_type=f32)
    nex = doc_lengths.shape[0]

    buf, narrow = pl.pallas_call(
        functools.partial(gather_kernel, nz, half),
        out_shape=(
            jax.ShapeDtypeStruct((half, npipe, CAP, width), b16),
            jax.ShapeDtypeStruct((CAP, 2 * rank), f32),
        ),
        in_specs=[VMEM] * 4,
        out_specs=(VMEM, VMEM),
        scratch_shapes=[
            pltpu.VMEM((CAP, width), b16),
            dma((3, PIECES)),
            dma((half, npipe, PIECES)),
            dma((half, npipe, PIECES)),
        ],
        compiler_params=params(0),
        name="gather",
    )(pick, grad_out, x_in, proj_in)

    wide = pl.pallas_call(
        functools.partial(hidden_kernel, tiles, half),
        grid=(tiles + 1,),
        out_shape=jax.ShapeDtypeStruct((3, CAP, rank), f32),
        in_specs=[
            pl.BlockSpec((half, npipe, CAP, width), lambda i: (0, 0, 0, 0)),
            pl.BlockSpec((tile, half * width), lambda i: (jnp.minimum(i, tiles - 1), 0)),
            pl.BlockSpec((tokens, tile), lambda i: (0, jnp.maximum(i - 1, 0))),
            pl.BlockSpec((tokens, tile), lambda i: (0, jnp.maximum(i - 1, 0))),
            pl.BlockSpec((tile, rank), lambda i: (jnp.maximum(i - 1, 0), 0)),
            pl.BlockSpec((CAP, tokens), lambda i: (0, 0)),
        ],
        out_specs=pl.BlockSpec((3, CAP, rank), lambda i: (0, 0, 0)),
        scratch_shapes=[
            pltpu.VMEM((2, CAP, tile), f32),
            pltpu.VMEM((tiles, CAP, tile), b16),
            pltpu.VMEM((tiles, CAP, tile), b16),
            dma((tiles,)),
            dma((tiles,)),
        ],
        compiler_params=params(1, dimension_semantics=("arbitrary",)),
        name="hidden",
    )(buf, w_down, gate_pre, up_pre, proj_ff, pick)

    partials = jnp.concatenate(
        [wide[0], wide[1], wide[2], narrow, jnp.zeros((CAP, rank), f32)], axis=1
    ).reshape(nz, CAP // nz, 6 * rank)
    shape = (nz, CAP // nz, 6 * rank)
    projected = pl.pallas_call(
        functools.partial(tensor_sum_kernel, nz),
        out_shape=jax.ShapeDtypeStruct(shape, f32),
        in_specs=[VMEM],
        out_specs=VMEM,
        scratch_shapes=[pltpu.VMEM(shape, f32)] + [dma((nz,))] * 4,
        compiler_params=params(2),
        name="tensor_sum",
    )(partials).reshape(CAP, 6 * rank)

    a_down, b_wide = projected[:, :rank], projected[:, rank : 3 * rank]
    a_in, b_down = projected[:, 3 * rank : 4 * rank], projected[:, 4 * rank : 5 * rank]

    def grads(left, right):
        masked = (member[:, :, None] * left[:, None, :]).reshape(CAP, nex * rank)
        return lax.dot_general(
            masked,
            right,
            (((0,), (0,)), ((), ())),
            precision=lax.Precision.HIGHEST,
            preferred_element_type=f32,
        ).reshape(nex, rank, right.shape[1])

    first = grads(a_down, b_down)
    rest = grads(a_in, b_wide)
    whole = jnp.stack([first, rest[..., :rank], rest[..., rank:]], axis=1).reshape(nex, -1)
    kron_part = bank_grads.shape[2]
    mine = lax.dynamic_slice_in_dim(
        whole, lax.axis_index("tensor") * kron_part, kron_part, axis=1
    )

    def small_sum(part, axes, cid, count=None, count_axes=None):
        n = int(np.prod([lax.axis_size(a) for a in axes]))
        outs = [jax.ShapeDtypeStruct(part.shape, f32)]
        scratch = [pltpu.VMEM((n,) + part.shape, f32), dma((n,)), dma((n,))]
        operands = [part]
        if count_axes:
            cn = int(np.prod([lax.axis_size(a) for a in count_axes]))
            outs.append(jax.ShapeDtypeStruct((cn,) + count.shape, f32))
            scratch += [dma((cn,)), dma((cn,))]
            operands.append(count)
        return pl.pallas_call(
            functools.partial(small_sum_kernel, axes, count_axes),
            out_shape=tuple(outs),
            in_specs=[VMEM] * len(operands),
            out_specs=(VMEM,) * len(outs),
            scratch_shapes=scratch,
            compiler_params=params(cid),
            name="small_sum",
        )(*operands)

    example_grads, counts = small_sum(
        mine,
        ("bank", "pipe"),
        3,
        jnp.full((8, 128), taken, f32),
        ("groups", "bank", "pipe"),
    )
    partial_value = lax.dot_general(
        example_grads,
        bank_grads[0].astype(f32),
        LAST,
        precision=lax.Precision.HIGHEST,
        preferred_element_type=f32,
    )
    owned = (owner == lax.axis_index("bank")).astype(f32)[:, None]
    (scores,) = small_sum(partial_value * owned, ("tensor", "bank"), 4)
    return lax.cond(
        jnp.max(counts) > CAP,
        lambda: body(
            x_in,
            grad_out,
            gate_pre,
            up_pre,
            w_down,
            proj_in,
            proj_ff,
            resp_mask,
            doc_lengths,
            owner,
            bank_grads,
        ),
        lambda: scores,
    )


def choose(*args):
    nz = lax.axis_size("tensor")
    fits = (
        lax.axis_size("pipe") == 2
        and nz % 2 == 0
        and 2 < nz <= 8
        and args[0].shape[0] >= CAP
        and CAP % (8 * nz) == 0
        and args[0].shape[1] % 128 == 0
        and args[2].shape[1] % 256 == 0
        and args[5].shape[1] == 64
    )
    return packed_body(*args) if fits else body(*args)


def solution(mesh):
    return jax.shard_map(
        choose,
        mesh=mesh,
        in_specs=(
            P(("groups", "bank", "pipe"), "tensor"),
            P(("groups", "bank", "pipe"), "tensor"),
            P(("groups", "bank", "pipe"), "tensor"),
            P(("groups", "bank", "pipe"), "tensor"),
            P("tensor", "pipe"),
            P("tensor", None),
            P("tensor", None),
            P(("groups", "bank", "pipe")),
            P("groups"),
            P("groups"),
            P("bank", "pipe", "tensor"),
        ),
        out_specs=P("groups", "pipe"),
        check_vma=False,
    )
```

```python
import functools
import jax
import jax.numpy as jnp
import numpy as np
from jax import lax
from jax.sharding import PartitionSpec as P
from jax.experimental import pallas as pl
from jax.experimental.pallas import tpu as pltpu

MESH = pl.DeviceIdType.MESH
VMEM = pl.BlockSpec(memory_space=pltpu.VMEM)
CAP = 320
PIECES = 4
LIMIT = 60 * 1024 * 1024
LAST = (((1,), (1,)), ((), ()))


def body(
    x_in,
    grad_out,
    gate_pre,
    up_pre,
    w_down,
    proj_in,
    proj_ff,
    resp_mask,
    doc_lengths,
    owner,
    bank_grads,
):
    rows_here = x_in.shape[0]
    proj_rank = proj_in.shape[1]
    contract_last = (((1,), (1,)), ((), ()))
    full_rows = lax.all_gather(grad_out, "tensor", axis=1, tiled=True)
    paired = lax.all_to_all(full_rows, "pipe", split_axis=1, concat_axis=0, tiled=True)
    hidden_grad = lax.psum_scatter(
        lax.dot_general(paired, w_down, contract_last, preferred_element_type=jnp.float32),
        "pipe",
        scatter_dimension=0,
        tiled=True,
    )
    gate_val = gate_pre.astype(jnp.float32)
    up_val = up_pre.astype(jnp.float32)
    sigmoid_gate = jax.nn.sigmoid(gate_val)
    activated = gate_val * sigmoid_gate
    slope = sigmoid_gate * (1.0 + gate_val * (1.0 - sigmoid_gate))
    hidden = (activated * up_val).astype(jnp.bfloat16)
    up_grad = (hidden_grad * activated).astype(jnp.bfloat16)
    gate_grad = (hidden_grad * up_val * slope).astype(jnp.bfloat16)
    wide_side = jnp.stack([hidden, up_grad, gate_grad])
    wide_proj = jnp.einsum("stf,fr->srt", wide_side, proj_ff, preferred_element_type=jnp.float32)
    narrow_side = jnp.stack([x_in, grad_out])
    narrow_proj = jnp.einsum(
        "std,dr->srt", narrow_side, proj_in, preferred_element_type=jnp.float32
    )
    partials = jnp.concatenate([wide_proj, narrow_proj], axis=0)
    projected = lax.psum(partials, "tensor")
    stacked = projected.reshape(5 * proj_rank, rows_here)
    kron_part = bank_grads.shape[2]
    square = proj_rank * proj_rank
    module_ids = np.repeat(np.arange(3), square)
    inner_ids = np.arange(3 * square) % square
    left_table = np.array([0, 3, 3])[module_ids] * proj_rank + inner_ids // proj_rank
    right_table = np.array([4, 1, 2])[module_ids] * proj_rank + inner_ids % proj_rank
    first_entry = lax.axis_index("tensor") * kron_part
    left_ids = lax.dynamic_slice_in_dim(jnp.asarray(left_table, jnp.int32), first_entry, kron_part)
    right_ids = lax.dynamic_slice_in_dim(
        jnp.asarray(right_table, jnp.int32), first_entry, kron_part
    )
    products = jnp.take(stacked, left_ids, axis=0) * jnp.take(stacked, right_ids, axis=0)
    offset = lax.axis_index(("bank", "pipe")) * rows_here
    positions = offset + jnp.arange(rows_here, dtype=jnp.int32)
    doc_ends = jnp.cumsum(doc_lengths)
    starts = doc_ends - doc_lengths
    inside = (positions[:, None] >= starts[None, :]) & (positions[:, None] < doc_ends[None, :])
    member = inside.astype(jnp.float32) * resp_mask.astype(jnp.float32)[:, None]
    grad_part = lax.dot_general(
        member,
        products,
        (((0,), (1,)), ((), ())),
        precision=lax.Precision.HIGHEST,
        preferred_element_type=jnp.float32,
    )
    example_grads = lax.psum(grad_part, ("bank", "pipe"))
    own_rows = bank_grads[0].astype(jnp.float32)
    partial_value = lax.dot_general(
        example_grads,
        own_rows,
        contract_last,
        precision=lax.Precision.HIGHEST,
        preferred_element_type=jnp.float32,
    )
    owned = (owner == lax.axis_index("bank")).astype(jnp.float32)[:, None]
    scores = lax.psum(partial_value * owned, ("tensor", "bank"))
    return scores


def params(cid, **more):
    return pltpu.CompilerParams(
        collective_id=cid, has_side_effects=True, vmem_limit_bytes=LIMIT, **more
    )


def greet(devices):
    barrier = pltpu.get_barrier_semaphore()
    for device in devices:
        pl.semaphore_signal(barrier, inc=1, device_id=device, device_id_type=MESH)
    pl.semaphore_wait(barrier, len(devices))


def layer_kernel(
    nz,
    half,
    tiles,
    tile,
    pick,
    grad,
    x_in,
    proj_in,
    proj_ff,
    weight,
    gate,
    up,
    wide,
    narrow,
    buf,
    packed,
    held,
    gate_in,
    up_in,
    act,
    rate,
    mine,
    sent,
    got,
    own_sem,
    fwd_sem,
    recv_sem,
    held_sem,
    gate_sem,
    up_sem,
    send_sem,
    got_sem,
):
    z, c = lax.axis_index("tensor"), lax.axis_index("pipe")
    other = 1 - c
    dest, place = z // half, z % half
    rank = proj_in.shape[0]
    width = packed.shape[1]
    rows = packed.shape[0] // PIECES
    part_rows = packed.shape[0] // 2
    events = 2 * half
    barrier = pltpu.get_barrier_semaphore()
    pl.semaphore_signal(barrier, inc=1, device_id={"pipe": other}, device_id_type=MESH)
    for step in (-1, 1):

        @pl.when((z + step >= 0) & (z + step < nz))
        def _():
            for core in range(2):
                pl.semaphore_signal(
                    barrier,
                    inc=1,
                    device_id={"tensor": z + step, "pipe": core},
                    device_id_type=MESH,
                )

    def columns(t):
        return pl.ds(pl.multiple_of(t * tile, tile), tile)

    def hold(t):
        return pltpu.make_async_copy(weight.at[columns(t)], held.at[t], held_sem.at[t])

    def fetch(t, do):
        slot = t % 2
        do(pltpu.make_async_copy(gate.at[:, columns(t)], gate_in.at[slot], gate_sem.at[slot]))
        do(pltpu.make_async_copy(up.at[:, columns(t)], up_in.at[slot], up_sem.at[slot]))

    fetch(0, lambda d: d.start())
    fetch(1, lambda d: d.start())
    packed[...] = jnp.dot(pick[...], grad[...], preferred_element_type=jnp.float32).astype(
        jnp.bfloat16
    )
    pl.semaphore_wait(barrier, jnp.where((z > 0) & (z < nz - 1), 5, 3))

    def piece(q):
        return pl.ds(pl.multiple_of(q * rows, 16), rows)

    def own(way, q):
        return pltpu.make_async_remote_copy(
            src_ref=packed.at[piece(q)],
            dst_ref=buf.at[place, c, piece(q)],
            send_sem=own_sem.at[way, q],
            recv_sem=recv_sem.at[place, c, q],
            device_id={"tensor": z + (1, -1, 0)[way], "pipe": dest},
            device_id_type=MESH,
        )

    goes = (z < nz - 1, z > 0, dest != c)

    for q in range(PIECES):
        for way in range(3):

            @pl.when(goes[way])
            def _():
                own(way, q).start()

    @pl.loop(0, tiles)
    def _(t):
        hold(t).start()

    @pl.when(dest == c)
    def _():
        buf[place, c] = packed[...]

    packed_x = jnp.dot(pick[...], x_in[...], preferred_element_type=jnp.float32).astype(
        jnp.bfloat16
    )
    narrow[:, 0:rank] = lax.dot_general(
        packed_x, proj_in[...], LAST, preferred_element_type=jnp.float32
    )
    narrow[:, rank : 2 * rank] = lax.dot_general(
        packed[...], proj_in[...], LAST, preferred_element_type=jnp.float32
    )
    wide[...] = jnp.zeros_like(wide)

    def passed(j, k, q, step):
        return pltpu.make_async_remote_copy(
            src_ref=buf.at[j, k, piece(q)],
            dst_ref=buf.at[j, k, piece(q)],
            send_sem=fwd_sem.at[j, k, q],
            recv_sem=recv_sem.at[j, k, q],
            device_id={"tensor": z + step, "pipe": c},
            device_id_type=MESH,
        )

    def event(e):
        q, i, k = e // events, (e // 2) % half, e % 2
        j = c * i + (1 - c) * (half - 1 - i)
        return j, k, q, c * half + j

    def receive(e):
        j, k, q, source = event(e)

        @pl.when((source != z) | (k != c))
        def _():
            passed(j, k, q, 0).wait_recv()

        @pl.when((source < z) & (z < nz - 1))
        def _():
            passed(j, k, q, 1).start()

        @pl.when((source > z) & (z > 0))
        def _():
            passed(j, k, q, -1).start()

    @pl.loop(0, tiles)
    def _(t):
        slot = t % 2
        fetch(t, lambda d: d.wait())
        gate_val = jnp.dot(pick[...], gate_in[slot], preferred_element_type=jnp.float32)
        up_val = jnp.dot(pick[...], up_in[slot], preferred_element_type=jnp.float32)

        @pl.when(t + 2 < tiles)
        def _():
            fetch(t + 2, lambda d: d.start())

        sig = jax.nn.sigmoid(gate_val)
        silu = gate_val * sig
        act[t] = silu
        rate[t] = up_val * (sig * (1.0 + gate_val * (1.0 - sig)))
        wide[0] += lax.dot_general(
            (silu * up_val).astype(jnp.bfloat16),
            proj_ff[:, columns(t)],
            LAST,
            preferred_element_type=jnp.float32,
        )

        @pl.when((t % 4 == 3) & (t // 4 < events))
        def _():
            receive(t // 4)

    early = min(events, tiles // 4)
    middle = events * PIECES // 2

    @pl.loop(early, middle)
    def _(e):
        receive(e)

    def copy(s):
        return pltpu.make_async_remote_copy(
            src_ref=sent.at[s],
            dst_ref=got.at[s],
            send_sem=send_sem.at[s],
            recv_sem=got_sem.at[s],
            device_id={"pipe": other},
            device_id_type=MESH,
        )

    def rows_of(s):
        return pl.ds(pl.multiple_of((s // tiles) * part_rows, 16), part_rows)

    def multiply(s):
        t, these = s % tiles, rows_of(s)
        total = None
        for j in range(half):
            left = jnp.concatenate([buf[j, other, these], buf[j, c, these]], axis=0)
            term = lax.dot_general(
                left,
                held[t, :, j * width : (j + 1) * width],
                LAST,
                preferred_element_type=jnp.float32,
            )
            total = term if total is None else total + term
        sent[s] = total[:part_rows].astype(jnp.bfloat16)
        copy(s).start()
        mine[s % 2] = total[part_rows:]

    def finish(s):
        t, these = s % tiles, rows_of(s)
        copy(s).wait_recv()
        hidden_grad = mine[s % 2] + got[s].astype(jnp.float32)
        table = proj_ff[:, columns(t)]
        for index, factor in ((1, act), (2, rate)):
            wide[index, these] += lax.dot_general(
                (hidden_grad * factor[t, these]).astype(jnp.bfloat16),
                table,
                LAST,
                preferred_element_type=jnp.float32,
            )

    @pl.loop(0, tiles)
    def _(s):
        hold(s).wait()
        multiply(s)

        @pl.when(s > 0)
        def _():
            finish(s - 1)

        @pl.when((s % 2 == 1) & (s // 2 < middle))
        def _():
            receive(middle + s // 2)

    for e in range(tiles // 2, middle):
        receive(middle + e)

    @pl.loop(tiles, 2 * tiles)
    def _(s):
        multiply(s)
        finish(s - 1)

    finish(2 * tiles - 1)

    @pl.loop(0, 2 * tiles)
    def _(s):
        copy(s).wait_send()

    for q in range(PIECES):
        for way in range(3):

            @pl.when(goes[way])
            def _():
                own(way, q).wait_send()

    @pl.loop(0, events * PIECES)
    def _(e):
        j, k, q, source = event(e)

        @pl.when(((source < z) & (z < nz - 1)) | ((source > z) & (z > 0)))
        def _():
            passed(j, k, q, 0).wait_send()


def tensor_sum_kernel(n, part, out, got, send_sem, recv_sem, send2, recv2):
    me = lax.axis_index("tensor")
    peers = [lax.rem(me + d, n) for d in range(1, n)]
    greet([{"tensor": peer} for peer in peers])

    def first(peer, slot):
        return pltpu.make_async_remote_copy(
            src_ref=part.at[peer],
            dst_ref=got.at[slot],
            send_sem=send_sem.at[peer],
            recv_sem=recv_sem.at[slot],
            device_id={"tensor": peer},
            device_id_type=MESH,
        )

    def second(peer, slot):
        return pltpu.make_async_remote_copy(
            src_ref=out.at[slot],
            dst_ref=out.at[slot],
            send_sem=send2.at[peer],
            recv_sem=recv2.at[slot],
            device_id={"tensor": peer},
            device_id_type=MESH,
        )

    for peer in peers:
        first(peer, me).start()
    got[me] = part[me]
    for peer in peers:
        first(peer, peer).wait_recv()
    total = got[0]
    for k in range(1, n):
        total = total + got[k]
    out[me] = total
    for peer in peers:
        second(peer, me).start()
    for peer in peers:
        second(peer, peer).wait_recv()
    for peer in peers:
        first(peer, me).wait_send()
        second(peer, me).wait_send()


def small_sum_kernel(axes, count_axes, *refs):
    if count_axes:
        part, count, out, counts, got, send_sem, recv_sem, csend, crecv = refs
    else:
        part, out, got, send_sem, recv_sem = refs

    def layout(names):
        sizes = [lax.axis_size(a) for a in names]
        me = lax.axis_index(names[0])
        for name, size in zip(names[1:], sizes[1:]):
            me = me * size + lax.axis_index(name)
        n = int(np.prod(sizes))
        peers = []
        for d in range(1, n):
            flat = lax.rem(me + d, n)
            rest, device = flat, {}
            for name, size in reversed(list(zip(names, sizes))):
                device[name] = lax.rem(rest, size)
                rest = rest // size
            peers.append((flat, device))
        return n, me, peers

    n, me, peers = layout(axes)

    def copy(flat, device, slot):
        return pltpu.make_async_remote_copy(
            src_ref=part,
            dst_ref=got.at[slot],
            send_sem=send_sem.at[flat],
            recv_sem=recv_sem.at[slot],
            device_id=device,
            device_id_type=MESH,
        )

    if count_axes:
        cn, cme, cpeers = layout(count_axes)

        def ccopy(flat, device, slot):
            return pltpu.make_async_remote_copy(
                src_ref=count,
                dst_ref=counts.at[slot],
                send_sem=csend.at[flat],
                recv_sem=crecv.at[slot],
                device_id=device,
                device_id_type=MESH,
            )

        greet([device for _, device in cpeers])
    else:
        greet([device for _, device in peers])
    for flat, device in peers:
        copy(flat, device, me).start()
    if count_axes:
        for flat, device in cpeers:
            ccopy(flat, device, cme).start()
        counts[cme] = count[...]
    got[me] = part[...]
    for flat, device in peers:
        copy(flat, device, flat).wait_recv()
    total = got[0]
    for k in range(1, n):
        total = total + got[k]
    out[...] = total
    for flat, device in peers:
        copy(flat, device, me).wait_send()
    if count_axes:
        for flat, device in cpeers:
            ccopy(flat, device, flat).wait_recv()
        for flat, device in cpeers:
            ccopy(flat, device, cme).wait_send()


def packed_body(
    x_in,
    grad_out,
    gate_pre,
    up_pre,
    w_down,
    proj_in,
    proj_ff,
    resp_mask,
    doc_lengths,
    owner,
    bank_grads,
):
    nz, npipe = lax.axis_size("tensor"), lax.axis_size("pipe")
    half = nz // npipe
    tokens, width = grad_out.shape
    hidden_units = gate_pre.shape[1]
    rank = proj_in.shape[1]
    tile = 256
    tiles = hidden_units // tile
    f32, b16 = jnp.float32, jnp.bfloat16
    dma = pltpu.SemaphoreType.DMA

    order = jnp.cumsum(resp_mask) - 1
    taken = jnp.sum(resp_mask)
    pick = ((order[None, :] == jnp.arange(CAP)[:, None]) & (resp_mask[None, :] > 0)).astype(b16)
    offset = lax.axis_index(("bank", "pipe")) * tokens
    positions = offset + jnp.arange(tokens, dtype=jnp.int32)
    doc_ends = jnp.cumsum(doc_lengths)
    starts = doc_ends - doc_lengths
    inside = (positions[:, None] >= starts[None, :]) & (positions[:, None] < doc_ends[None, :])
    member = jnp.dot(pick, inside.astype(b16), preferred_element_type=f32)
    nex = doc_lengths.shape[0]

    any_place = pl.BlockSpec(memory_space=pl.ANY)
    wide, narrow = pl.pallas_call(
        functools.partial(layer_kernel, nz, half, tiles, tile),
        out_shape=(
            jax.ShapeDtypeStruct((3, CAP, rank), f32),
            jax.ShapeDtypeStruct((CAP, 2 * rank), f32),
        ),
        in_specs=[VMEM] * 5 + [any_place] * 3,
        out_specs=(VMEM, VMEM),
        scratch_shapes=[
            pltpu.VMEM((half, npipe, CAP, width), b16),
            pltpu.VMEM((CAP, width), b16),
            pltpu.VMEM((tiles, tile, half * width), b16),
            pltpu.VMEM((2, tokens, tile), b16),
            pltpu.VMEM((2, tokens, tile), b16),
            pltpu.VMEM((tiles, CAP, tile), f32),
            pltpu.VMEM((tiles, CAP, tile), f32),
            pltpu.VMEM((2, CAP // 2, tile), f32),
            pltpu.VMEM((2 * tiles, CAP // 2, tile), b16),
            pltpu.VMEM((2 * tiles, CAP // 2, tile), b16),
            dma((3, PIECES)),
            dma((half, npipe, PIECES)),
            dma((half, npipe, PIECES)),
            dma((tiles,)),
            dma((2,)),
            dma((2,)),
            dma((2 * tiles,)),
            dma((2 * tiles,)),
        ],
        compiler_params=params(0),
        name="layer",
    )(pick, grad_out, x_in, proj_in.T, proj_ff.T, w_down, gate_pre, up_pre)

    partials = jnp.concatenate(
        [wide[0], wide[1], wide[2], narrow, jnp.zeros((CAP, rank), f32)], axis=1
    ).reshape(nz, CAP // nz, 6 * rank)
    shape = (nz, CAP // nz, 6 * rank)
    projected = pl.pallas_call(
        functools.partial(tensor_sum_kernel, nz),
        out_shape=jax.ShapeDtypeStruct(shape, f32),
        in_specs=[VMEM],
        out_specs=VMEM,
        scratch_shapes=[pltpu.VMEM(shape, f32)] + [dma((nz,))] * 4,
        compiler_params=params(2),
        name="tensor_sum",
    )(partials).reshape(CAP, 6 * rank)

    a_down, b_wide = projected[:, :rank], projected[:, rank : 3 * rank]
    a_in, b_down = projected[:, 3 * rank : 4 * rank], projected[:, 4 * rank : 5 * rank]

    def grads(left, right):
        masked = (member[:, :, None] * left[:, None, :]).reshape(CAP, nex * rank)
        return lax.dot_general(
            masked,
            right,
            (((0,), (0,)), ((), ())),
            precision=lax.Precision.HIGHEST,
            preferred_element_type=f32,
        ).reshape(nex, rank, right.shape[1])

    first = grads(a_down, b_down)
    rest = grads(a_in, b_wide)
    whole = jnp.stack([first, rest[..., :rank], rest[..., rank:]], axis=1).reshape(nex, -1)
    kron_part = bank_grads.shape[2]
    mine = lax.dynamic_slice_in_dim(
        whole, lax.axis_index("tensor") * kron_part, kron_part, axis=1
    )

    def small_sum(part, axes, cid, count=None, count_axes=None):
        n = int(np.prod([lax.axis_size(a) for a in axes]))
        outs = [jax.ShapeDtypeStruct(part.shape, f32)]
        scratch = [pltpu.VMEM((n,) + part.shape, f32), dma((n,)), dma((n,))]
        operands = [part]
        if count_axes:
            cn = int(np.prod([lax.axis_size(a) for a in count_axes]))
            outs.append(jax.ShapeDtypeStruct((cn,) + count.shape, f32))
            scratch += [dma((cn,)), dma((cn,))]
            operands.append(count)
        return pl.pallas_call(
            functools.partial(small_sum_kernel, axes, count_axes),
            out_shape=tuple(outs),
            in_specs=[VMEM] * len(operands),
            out_specs=(VMEM,) * len(outs),
            scratch_shapes=scratch,
            compiler_params=params(cid),
            name="small_sum",
        )(*operands)

    example_grads, counts = small_sum(
        mine,
        ("bank", "pipe"),
        3,
        jnp.full((8, 128), taken, f32),
        ("groups", "bank", "pipe"),
    )
    partial_value = lax.dot_general(
        example_grads,
        bank_grads[0].astype(f32),
        LAST,
        precision=lax.Precision.HIGHEST,
        preferred_element_type=f32,
    )
    owned = (owner == lax.axis_index("bank")).astype(f32)[:, None]
    (scores,) = small_sum(partial_value * owned, ("tensor", "bank"), 4)
    return lax.cond(
        jnp.max(counts) > CAP,
        lambda: body(
            x_in,
            grad_out,
            gate_pre,
            up_pre,
            w_down,
            proj_in,
            proj_ff,
            resp_mask,
            doc_lengths,
            owner,
            bank_grads,
        ),
        lambda: scores,
    )


def choose(*args):
    nz = lax.axis_size("tensor")
    fits = (
        lax.axis_size("pipe") == 2
        and nz % 2 == 0
        and 2 < nz <= 8
        and args[0].shape[0] >= CAP
        and CAP % (8 * nz) == 0
        and args[0].shape[1] % 128 == 0
        and args[2].shape[1] % 256 == 0
        and args[5].shape[1] == 64
    )
    return packed_body(*args) if fits else body(*args)


def solution(mesh):
    return jax.shard_map(
        choose,
        mesh=mesh,
        in_specs=(
            P(("groups", "bank", "pipe"), "tensor"),
            P(("groups", "bank", "pipe"), "tensor"),
            P(("groups", "bank", "pipe"), "tensor"),
            P(("groups", "bank", "pipe"), "tensor"),
            P("tensor", "pipe"),
            P("tensor", None),
            P("tensor", None),
            P(("groups", "bank", "pipe")),
            P("groups"),
            P("groups"),
            P("bank", "pipe", "tensor"),
        ),
        out_specs=P("groups", "pipe"),
        check_vma=False,
    )
```

```python
import functools
import jax
import jax.numpy as jnp
import numpy as np
from jax import lax
from jax.sharding import PartitionSpec as P
from jax.experimental import pallas as pl
from jax.experimental.pallas import tpu as pltpu

MESH = pl.DeviceIdType.MESH
VMEM = pl.BlockSpec(memory_space=pltpu.VMEM)
CAP = 320
PIECES = 4
LAG = 4
LIMIT = 60 * 1024 * 1024
LAST = (((1,), (1,)), ((), ()))


def body(
    x_in,
    grad_out,
    gate_pre,
    up_pre,
    w_down,
    proj_in,
    proj_ff,
    resp_mask,
    doc_lengths,
    owner,
    bank_grads,
):
    rows_here = x_in.shape[0]
    proj_rank = proj_in.shape[1]
    contract_last = (((1,), (1,)), ((), ()))
    full_rows = lax.all_gather(grad_out, "tensor", axis=1, tiled=True)
    paired = lax.all_to_all(full_rows, "pipe", split_axis=1, concat_axis=0, tiled=True)
    hidden_grad = lax.psum_scatter(
        lax.dot_general(paired, w_down, contract_last, preferred_element_type=jnp.float32),
        "pipe",
        scatter_dimension=0,
        tiled=True,
    )
    gate_val = gate_pre.astype(jnp.float32)
    up_val = up_pre.astype(jnp.float32)
    sigmoid_gate = jax.nn.sigmoid(gate_val)
    activated = gate_val * sigmoid_gate
    slope = sigmoid_gate * (1.0 + gate_val * (1.0 - sigmoid_gate))
    hidden = (activated * up_val).astype(jnp.bfloat16)
    up_grad = (hidden_grad * activated).astype(jnp.bfloat16)
    gate_grad = (hidden_grad * up_val * slope).astype(jnp.bfloat16)
    wide_side = jnp.stack([hidden, up_grad, gate_grad])
    wide_proj = jnp.einsum("stf,fr->srt", wide_side, proj_ff, preferred_element_type=jnp.float32)
    narrow_side = jnp.stack([x_in, grad_out])
    narrow_proj = jnp.einsum(
        "std,dr->srt", narrow_side, proj_in, preferred_element_type=jnp.float32
    )
    partials = jnp.concatenate([wide_proj, narrow_proj], axis=0)
    projected = lax.psum(partials, "tensor")
    stacked = projected.reshape(5 * proj_rank, rows_here)
    kron_part = bank_grads.shape[2]
    square = proj_rank * proj_rank
    module_ids = np.repeat(np.arange(3), square)
    inner_ids = np.arange(3 * square) % square
    left_table = np.array([0, 3, 3])[module_ids] * proj_rank + inner_ids // proj_rank
    right_table = np.array([4, 1, 2])[module_ids] * proj_rank + inner_ids % proj_rank
    first_entry = lax.axis_index("tensor") * kron_part
    left_ids = lax.dynamic_slice_in_dim(jnp.asarray(left_table, jnp.int32), first_entry, kron_part)
    right_ids = lax.dynamic_slice_in_dim(
        jnp.asarray(right_table, jnp.int32), first_entry, kron_part
    )
    products = jnp.take(stacked, left_ids, axis=0) * jnp.take(stacked, right_ids, axis=0)
    offset = lax.axis_index(("bank", "pipe")) * rows_here
    positions = offset + jnp.arange(rows_here, dtype=jnp.int32)
    doc_ends = jnp.cumsum(doc_lengths)
    starts = doc_ends - doc_lengths
    inside = (positions[:, None] >= starts[None, :]) & (positions[:, None] < doc_ends[None, :])
    member = inside.astype(jnp.float32) * resp_mask.astype(jnp.float32)[:, None]
    grad_part = lax.dot_general(
        member,
        products,
        (((0,), (1,)), ((), ())),
        precision=lax.Precision.HIGHEST,
        preferred_element_type=jnp.float32,
    )
    example_grads = lax.psum(grad_part, ("bank", "pipe"))
    own_rows = bank_grads[0].astype(jnp.float32)
    partial_value = lax.dot_general(
        example_grads,
        own_rows,
        contract_last,
        precision=lax.Precision.HIGHEST,
        preferred_element_type=jnp.float32,
    )
    owned = (owner == lax.axis_index("bank")).astype(jnp.float32)[:, None]
    scores = lax.psum(partial_value * owned, ("tensor", "bank"))
    return scores


def params(cid, **more):
    return pltpu.CompilerParams(
        collective_id=cid, has_side_effects=True, vmem_limit_bytes=LIMIT, **more
    )


def greet(devices):
    barrier = pltpu.get_barrier_semaphore()
    for device in devices:
        pl.semaphore_signal(barrier, inc=1, device_id=device, device_id_type=MESH)
    pl.semaphore_wait(barrier, len(devices))


def layer_kernel(
    nz,
    half,
    tiles,
    tile,
    pick,
    grad,
    x_in,
    proj_in,
    proj_ff,
    weight,
    gate,
    up,
    part,
    wide,
    narrow,
    buf,
    packed,
    held,
    gate_in,
    up_in,
    act,
    rate,
    mine,
    sent,
    got,
    own_sem,
    fwd_sem,
    recv_sem,
    held_sem,
    gate_sem,
    up_sem,
    send_sem,
    got_sem,
):
    z, c = lax.axis_index("tensor"), lax.axis_index("pipe")
    other = 1 - c
    dest, place = z // half, z % half
    rank = proj_in.shape[0]
    width = packed.shape[1]
    rows = packed.shape[0] // PIECES
    part_rows = packed.shape[0] // 2
    events = 2 * half
    barrier = pltpu.get_barrier_semaphore()
    pl.semaphore_signal(barrier, inc=1, device_id={"pipe": other}, device_id_type=MESH)
    for step in (-1, 1):

        @pl.when((z + step >= 0) & (z + step < nz))
        def _():
            for core in range(2):
                pl.semaphore_signal(
                    barrier,
                    inc=1,
                    device_id={"tensor": z + step, "pipe": core},
                    device_id_type=MESH,
                )

    def columns(t):
        return pl.ds(pl.multiple_of(t * tile, tile), tile)

    def hold(t):
        return pltpu.make_async_copy(weight.at[columns(t)], held.at[t], held_sem.at[t])

    def fetch(t, do):
        slot = t % 2
        do(pltpu.make_async_copy(gate.at[:, columns(t)], gate_in.at[slot], gate_sem.at[slot]))
        do(pltpu.make_async_copy(up.at[:, columns(t)], up_in.at[slot], up_sem.at[slot]))

    fetch(0, lambda d: d.start())
    fetch(1, lambda d: d.start())
    packed[...] = jnp.dot(pick[...], grad[...], preferred_element_type=jnp.float32).astype(
        jnp.bfloat16
    )
    pl.semaphore_wait(barrier, jnp.where((z > 0) & (z < nz - 1), 5, 3))

    def piece(q):
        return pl.ds(pl.multiple_of(q * rows, 16), rows)

    def own(way, q):
        return pltpu.make_async_remote_copy(
            src_ref=packed.at[piece(q)],
            dst_ref=buf.at[place, c, piece(q)],
            send_sem=own_sem.at[way, q],
            recv_sem=recv_sem.at[place, c, q],
            device_id={"tensor": z + (1, -1, 0)[way], "pipe": dest},
            device_id_type=MESH,
        )

    goes = (z < nz - 1, z > 0, dest != c)

    for q in range(PIECES):
        for way in range(3):

            @pl.when(goes[way])
            def _():
                own(way, q).start()

    @pl.loop(0, tiles)
    def _(t):
        hold(t).start()

    @pl.when(dest == c)
    def _():
        buf[place, c] = packed[...]

    packed_x = jnp.dot(pick[...], x_in[...], preferred_element_type=jnp.float32).astype(
        jnp.bfloat16
    )
    narrow[:, 0:rank] = lax.dot_general(
        packed_x, proj_in[...], LAST, preferred_element_type=jnp.float32
    )
    narrow[:, rank : 2 * rank] = lax.dot_general(
        packed[...], proj_in[...], LAST, preferred_element_type=jnp.float32
    )
    wide[...] = jnp.zeros_like(wide)

    def passed(j, k, q, step):
        return pltpu.make_async_remote_copy(
            src_ref=buf.at[j, k, piece(q)],
            dst_ref=buf.at[j, k, piece(q)],
            send_sem=fwd_sem.at[j, k, q],
            recv_sem=recv_sem.at[j, k, q],
            device_id={"tensor": z + step, "pipe": c},
            device_id_type=MESH,
        )

    def event(e):
        q, i, k = e // events, (e // 2) % half, e % 2
        j = c * i + (1 - c) * (half - 1 - i)
        return j, k, q, c * half + j

    def receive(e):
        j, k, q, source = event(e)

        @pl.when((source != z) | (k != c))
        def _():
            passed(j, k, q, 0).wait_recv()

        @pl.when((source < z) & (z < nz - 1))
        def _():
            passed(j, k, q, 1).start()

        @pl.when((source > z) & (z > 0))
        def _():
            passed(j, k, q, -1).start()

    @pl.loop(0, tiles)
    def _(t):
        slot = t % 2
        fetch(t, lambda d: d.wait())
        gate_val = jnp.dot(pick[...], gate_in[slot], preferred_element_type=jnp.float32)
        up_val = jnp.dot(pick[...], up_in[slot], preferred_element_type=jnp.float32)

        @pl.when(t + 2 < tiles)
        def _():
            fetch(t + 2, lambda d: d.start())

        sig = jax.nn.sigmoid(gate_val)
        silu = gate_val * sig
        act[t] = silu
        rate[t] = up_val * (sig * (1.0 + gate_val * (1.0 - sig)))
        wide[0] += lax.dot_general(
            (silu * up_val).astype(jnp.bfloat16),
            proj_ff[:, columns(t)],
            LAST,
            preferred_element_type=jnp.float32,
        )

        @pl.when((t % 4 == 3) & (t // 4 < events))
        def _():
            receive(t // 4)

    early = min(events, tiles // 4)
    middle = events * PIECES // 2

    @pl.loop(early, middle)
    def _(e):
        receive(e)

    def copy(s):
        return pltpu.make_async_remote_copy(
            src_ref=sent.at[s],
            dst_ref=got.at[s],
            send_sem=send_sem.at[s],
            recv_sem=got_sem.at[s],
            device_id={"pipe": other},
            device_id_type=MESH,
        )

    def rows_of(s):
        return pl.ds(pl.multiple_of((s // tiles) * part_rows, 16), part_rows)

    def multiply(s):
        t, these = s % tiles, rows_of(s)
        total = None
        for j in range(half):
            left = jnp.concatenate([buf[j, other, these], buf[j, c, these]], axis=0)
            term = lax.dot_general(
                left,
                held[t, :, j * width : (j + 1) * width],
                LAST,
                preferred_element_type=jnp.float32,
            )
            total = term if total is None else total + term
        sent[s] = total[:part_rows].astype(jnp.bfloat16)
        copy(s).start()
        mine[s % (2 * LAG)] = total[part_rows:]

    def finish(s):
        t, these = s % tiles, rows_of(s)
        copy(s).wait_recv()
        hidden_grad = mine[s % (2 * LAG)] + got[s].astype(jnp.float32)
        table = proj_ff[:, columns(t)]
        for index, factor in ((1, act), (2, rate)):
            wide[index, these] += lax.dot_general(
                (hidden_grad * factor[t, these]).astype(jnp.bfloat16),
                table,
                LAST,
                preferred_element_type=jnp.float32,
            )

    @pl.loop(0, tiles)
    def _(s):
        hold(s).wait()
        multiply(s)

        @pl.when(s >= LAG)
        def _():
            finish(s - LAG)

        @pl.when((s % 2 == 1) & (s // 2 < middle))
        def _():
            receive(middle + s // 2)

    for e in range(tiles // 2, middle):
        receive(middle + e)

    @pl.loop(tiles, 2 * tiles)
    def _(s):
        multiply(s)
        finish(s - LAG)

    @pl.loop(2 * tiles - LAG, 2 * tiles)
    def _(s):
        finish(s)

    block = packed.shape[0] // nz
    for k in range(nz):
        low, mid, high = k * block, k * block + block // 2, (k + 1) * block
        part[k, 0:block, 0:rank] = wide[0, low:high]
        part[k, 0:block, rank:] = wide[1, low:high]
        part[k, block : 2 * block, 0:rank] = wide[2, low:high]
        part[k, block : 2 * block, rank:] = narrow[low:high, 0:rank]
        part[k, 2 * block :, 0:rank] = narrow[low:mid, rank:]
        part[k, 2 * block :, rank:] = narrow[mid:high, rank:]

    @pl.loop(0, 2 * tiles)
    def _(s):
        copy(s).wait_send()

    for q in range(PIECES):
        for way in range(3):

            @pl.when(goes[way])
            def _():
                own(way, q).wait_send()

    @pl.loop(0, events * PIECES)
    def _(e):
        j, k, q, source = event(e)

        @pl.when(((source < z) & (z < nz - 1)) | ((source > z) & (z > 0)))
        def _():
            passed(j, k, q, 0).wait_send()


def tensor_sum_kernel(n, part, out, got, send_sem, recv_sem, send2, recv2):
    me = lax.axis_index("tensor")
    peers = [lax.rem(me + d, n) for d in range(1, n)]
    greet([{"tensor": peer} for peer in peers])

    def first(peer, slot):
        return pltpu.make_async_remote_copy(
            src_ref=part.at[peer],
            dst_ref=got.at[slot],
            send_sem=send_sem.at[peer],
            recv_sem=recv_sem.at[slot],
            device_id={"tensor": peer},
            device_id_type=MESH,
        )

    def second(peer, slot):
        return pltpu.make_async_remote_copy(
            src_ref=out.at[slot],
            dst_ref=out.at[slot],
            send_sem=send2.at[peer],
            recv_sem=recv2.at[slot],
            device_id={"tensor": peer},
            device_id_type=MESH,
        )

    for peer in peers:
        first(peer, me).start()
    got[me] = part[me]
    for peer in peers:
        first(peer, peer).wait_recv()
    total = got[0]
    for k in range(1, n):
        total = total + got[k]
    out[me] = total
    for peer in peers:
        second(peer, me).start()
    for peer in peers:
        second(peer, peer).wait_recv()
    for peer in peers:
        first(peer, me).wait_send()
        second(peer, me).wait_send()


def small_sum_kernel(axes, count_axes, *refs):
    if count_axes:
        part, count, out, counts, got, send_sem, recv_sem, csend, crecv = refs
    else:
        part, out, got, send_sem, recv_sem = refs

    def layout(names):
        sizes = [lax.axis_size(a) for a in names]
        me = lax.axis_index(names[0])
        for name, size in zip(names[1:], sizes[1:]):
            me = me * size + lax.axis_index(name)
        n = int(np.prod(sizes))
        peers = []
        for d in range(1, n):
            flat = lax.rem(me + d, n)
            rest, device = flat, {}
            for name, size in reversed(list(zip(names, sizes))):
                device[name] = lax.rem(rest, size)
                rest = rest // size
            peers.append((flat, device))
        return n, me, peers

    n, me, peers = layout(axes)

    def copy(flat, device, slot):
        return pltpu.make_async_remote_copy(
            src_ref=part,
            dst_ref=got.at[slot],
            send_sem=send_sem.at[flat],
            recv_sem=recv_sem.at[slot],
            device_id=device,
            device_id_type=MESH,
        )

    if count_axes:
        cn, cme, cpeers = layout(count_axes)

        def ccopy(flat, device, slot):
            return pltpu.make_async_remote_copy(
                src_ref=count,
                dst_ref=counts.at[slot],
                send_sem=csend.at[flat],
                recv_sem=crecv.at[slot],
                device_id=device,
                device_id_type=MESH,
            )

        greet([device for _, device in cpeers])
    else:
        greet([device for _, device in peers])
    for flat, device in peers:
        copy(flat, device, me).start()
    if count_axes:
        for flat, device in cpeers:
            ccopy(flat, device, cme).start()
        counts[cme] = count[...]
    got[me] = part[...]
    for flat, device in peers:
        copy(flat, device, flat).wait_recv()
    total = got[0]
    for k in range(1, n):
        total = total + got[k]
    out[...] = total
    for flat, device in peers:
        copy(flat, device, me).wait_send()
    if count_axes:
        for flat, device in cpeers:
            ccopy(flat, device, flat).wait_recv()
        for flat, device in cpeers:
            ccopy(flat, device, cme).wait_send()


def packed_body(
    x_in,
    grad_out,
    gate_pre,
    up_pre,
    w_down,
    proj_in,
    proj_ff,
    resp_mask,
    doc_lengths,
    owner,
    bank_grads,
):
    nz, npipe = lax.axis_size("tensor"), lax.axis_size("pipe")
    half = nz // npipe
    tokens, width = grad_out.shape
    hidden_units = gate_pre.shape[1]
    rank = proj_in.shape[1]
    tile = 256
    tiles = hidden_units // tile
    f32, b16 = jnp.float32, jnp.bfloat16
    dma = pltpu.SemaphoreType.DMA

    order = jnp.cumsum(resp_mask) - 1
    taken = jnp.sum(resp_mask)
    pick = ((order[None, :] == jnp.arange(CAP)[:, None]) & (resp_mask[None, :] > 0)).astype(b16)
    offset = lax.axis_index(("bank", "pipe")) * tokens
    positions = offset + jnp.arange(tokens, dtype=jnp.int32)
    doc_ends = jnp.cumsum(doc_lengths)
    starts = doc_ends - doc_lengths
    inside = (positions[:, None] >= starts[None, :]) & (positions[:, None] < doc_ends[None, :])
    member = jnp.dot(pick, inside.astype(b16), preferred_element_type=f32)
    nex = doc_lengths.shape[0]

    any_place = pl.BlockSpec(memory_space=pl.ANY)
    shape = (nz, 5 * CAP // (2 * nz), 2 * rank)
    partials = pl.pallas_call(
        functools.partial(layer_kernel, nz, half, tiles, tile),
        out_shape=jax.ShapeDtypeStruct(shape, f32),
        in_specs=[VMEM] * 5 + [any_place] * 3,
        out_specs=VMEM,
        scratch_shapes=[
            pltpu.VMEM((3, CAP, rank), f32),
            pltpu.VMEM((CAP, 2 * rank), f32),
            pltpu.VMEM((half, npipe, CAP, width), b16),
            pltpu.VMEM((CAP, width), b16),
            pltpu.VMEM((tiles, tile, half * width), b16),
            pltpu.VMEM((2, tokens, tile), b16),
            pltpu.VMEM((2, tokens, tile), b16),
            pltpu.VMEM((tiles, CAP, tile), f32),
            pltpu.VMEM((tiles, CAP, tile), f32),
            pltpu.VMEM((2 * LAG, CAP // 2, tile), f32),
            pltpu.VMEM((2 * tiles, CAP // 2, tile), b16),
            pltpu.VMEM((2 * tiles, CAP // 2, tile), b16),
            dma((3, PIECES)),
            dma((half, npipe, PIECES)),
            dma((half, npipe, PIECES)),
            dma((tiles,)),
            dma((2,)),
            dma((2,)),
            dma((2 * tiles,)),
            dma((2 * tiles,)),
        ],
        compiler_params=params(0),
        name="layer",
    )(pick, grad_out, x_in, proj_in.T, proj_ff.T, w_down, gate_pre, up_pre)

    projected = pl.pallas_call(
        functools.partial(tensor_sum_kernel, nz),
        out_shape=jax.ShapeDtypeStruct(shape, f32),
        in_specs=[VMEM],
        out_specs=VMEM,
        scratch_shapes=[pltpu.VMEM(shape, f32)] + [dma((nz,))] * 4,
        compiler_params=params(2),
        name="tensor_sum",
    )(partials)

    block = CAP // nz
    a_down = projected[:, :block, :rank].reshape(CAP, rank)
    b_up = projected[:, :block, rank:]
    b_gate = projected[:, block : 2 * block, :rank]
    b_wide = jnp.concatenate([b_up, b_gate], axis=2).reshape(CAP, 2 * rank)
    a_in = projected[:, block : 2 * block, rank:].reshape(CAP, rank)
    b_down = jnp.concatenate(
        [projected[:, 2 * block :, :rank], projected[:, 2 * block :, rank:]], axis=1
    ).reshape(CAP, rank)

    def grads(left, right):
        masked = (member[:, :, None] * left[:, None, :]).reshape(CAP, nex * rank)
        return lax.dot_general(
            masked,
            right,
            (((0,), (0,)), ((), ())),
            precision=lax.Precision.HIGHEST,
            preferred_element_type=f32,
        ).reshape(nex, rank, right.shape[1])

    first = grads(a_down, b_down)
    rest = grads(a_in, b_wide)
    whole = jnp.stack([first, rest[..., :rank], rest[..., rank:]], axis=1).reshape(nex, -1)
    kron_part = bank_grads.shape[2]
    mine = lax.dynamic_slice_in_dim(
        whole, lax.axis_index("tensor") * kron_part, kron_part, axis=1
    )

    def small_sum(part, axes, cid, count=None, count_axes=None):
        n = int(np.prod([lax.axis_size(a) for a in axes]))
        outs = [jax.ShapeDtypeStruct(part.shape, f32)]
        scratch = [pltpu.VMEM((n,) + part.shape, f32), dma((n,)), dma((n,))]
        operands = [part]
        if count_axes:
            cn = int(np.prod([lax.axis_size(a) for a in count_axes]))
            outs.append(jax.ShapeDtypeStruct((cn,) + count.shape, f32))
            scratch += [dma((cn,)), dma((cn,))]
            operands.append(count)
        return pl.pallas_call(
            functools.partial(small_sum_kernel, axes, count_axes),
            out_shape=tuple(outs),
            in_specs=[VMEM] * len(operands),
            out_specs=(VMEM,) * len(outs),
            scratch_shapes=scratch,
            compiler_params=params(cid),
            name="small_sum",
        )(*operands)

    example_grads, counts = small_sum(
        mine,
        ("bank", "pipe"),
        3,
        jnp.full((8, 128), taken, f32),
        ("groups", "bank", "pipe"),
    )
    partial_value = lax.dot_general(
        example_grads,
        bank_grads[0].astype(f32),
        LAST,
        precision=lax.Precision.HIGHEST,
        preferred_element_type=f32,
    )
    owned = (owner == lax.axis_index("bank")).astype(f32)[:, None]
    (scores,) = small_sum(partial_value * owned, ("tensor", "bank"), 4)
    return lax.cond(
        jnp.max(counts) > CAP,
        lambda: body(
            x_in,
            grad_out,
            gate_pre,
            up_pre,
            w_down,
            proj_in,
            proj_ff,
            resp_mask,
            doc_lengths,
            owner,
            bank_grads,
        ),
        lambda: scores,
    )


def choose(*args):
    nz = lax.axis_size("tensor")
    fits = (
        lax.axis_size("pipe") == 2
        and nz % 2 == 0
        and 2 < nz <= 8
        and args[0].shape[0] >= CAP
        and CAP % (16 * nz) == 0
        and args[0].shape[1] % 128 == 0
        and args[2].shape[1] % 256 == 0
        and args[5].shape[1] == 64
    )
    return packed_body(*args) if fits else body(*args)


def solution(mesh):
    return jax.shard_map(
        choose,
        mesh=mesh,
        in_specs=(
            P(("groups", "bank", "pipe"), "tensor"),
            P(("groups", "bank", "pipe"), "tensor"),
            P(("groups", "bank", "pipe"), "tensor"),
            P(("groups", "bank", "pipe"), "tensor"),
            P("tensor", "pipe"),
            P("tensor", None),
            P("tensor", None),
            P(("groups", "bank", "pipe")),
            P("groups"),
            P("groups"),
            P("bank", "pipe", "tensor"),
        ),
        out_specs=P("groups", "pipe"),
        check_vma=False,
    )
```

```python
import functools
import jax
import jax.numpy as jnp
import numpy as np
from jax import lax
from jax.sharding import PartitionSpec as P
from jax.experimental import pallas as pl
from jax.experimental.pallas import tpu as pltpu

MESH = pl.DeviceIdType.MESH
VMEM = pl.BlockSpec(memory_space=pltpu.VMEM)
CAP = 320
PIECES = 4
LAG = 4
LIMIT = 60 * 1024 * 1024
LAST = (((1,), (1,)), ((), ()))


def body(
    x_in,
    grad_out,
    gate_pre,
    up_pre,
    w_down,
    proj_in,
    proj_ff,
    resp_mask,
    doc_lengths,
    owner,
    bank_grads,
):
    rows_here = x_in.shape[0]
    proj_rank = proj_in.shape[1]
    contract_last = (((1,), (1,)), ((), ()))
    full_rows = lax.all_gather(grad_out, "tensor", axis=1, tiled=True)
    paired = lax.all_to_all(full_rows, "pipe", split_axis=1, concat_axis=0, tiled=True)
    hidden_grad = lax.psum_scatter(
        lax.dot_general(paired, w_down, contract_last, preferred_element_type=jnp.float32),
        "pipe",
        scatter_dimension=0,
        tiled=True,
    )
    gate_val = gate_pre.astype(jnp.float32)
    up_val = up_pre.astype(jnp.float32)
    sigmoid_gate = jax.nn.sigmoid(gate_val)
    activated = gate_val * sigmoid_gate
    slope = sigmoid_gate * (1.0 + gate_val * (1.0 - sigmoid_gate))
    hidden = (activated * up_val).astype(jnp.bfloat16)
    up_grad = (hidden_grad * activated).astype(jnp.bfloat16)
    gate_grad = (hidden_grad * up_val * slope).astype(jnp.bfloat16)
    wide_side = jnp.stack([hidden, up_grad, gate_grad])
    wide_proj = jnp.einsum("stf,fr->srt", wide_side, proj_ff, preferred_element_type=jnp.float32)
    narrow_side = jnp.stack([x_in, grad_out])
    narrow_proj = jnp.einsum(
        "std,dr->srt", narrow_side, proj_in, preferred_element_type=jnp.float32
    )
    partials = jnp.concatenate([wide_proj, narrow_proj], axis=0)
    projected = lax.psum(partials, "tensor")
    stacked = projected.reshape(5 * proj_rank, rows_here)
    kron_part = bank_grads.shape[2]
    square = proj_rank * proj_rank
    module_ids = np.repeat(np.arange(3), square)
    inner_ids = np.arange(3 * square) % square
    left_table = np.array([0, 3, 3])[module_ids] * proj_rank + inner_ids // proj_rank
    right_table = np.array([4, 1, 2])[module_ids] * proj_rank + inner_ids % proj_rank
    first_entry = lax.axis_index("tensor") * kron_part
    left_ids = lax.dynamic_slice_in_dim(jnp.asarray(left_table, jnp.int32), first_entry, kron_part)
    right_ids = lax.dynamic_slice_in_dim(
        jnp.asarray(right_table, jnp.int32), first_entry, kron_part
    )
    products = jnp.take(stacked, left_ids, axis=0) * jnp.take(stacked, right_ids, axis=0)
    offset = lax.axis_index(("bank", "pipe")) * rows_here
    positions = offset + jnp.arange(rows_here, dtype=jnp.int32)
    doc_ends = jnp.cumsum(doc_lengths)
    starts = doc_ends - doc_lengths
    inside = (positions[:, None] >= starts[None, :]) & (positions[:, None] < doc_ends[None, :])
    member = inside.astype(jnp.float32) * resp_mask.astype(jnp.float32)[:, None]
    grad_part = lax.dot_general(
        member,
        products,
        (((0,), (1,)), ((), ())),
        precision=lax.Precision.HIGHEST,
        preferred_element_type=jnp.float32,
    )
    example_grads = lax.psum(grad_part, ("bank", "pipe"))
    own_rows = bank_grads[0].astype(jnp.float32)
    partial_value = lax.dot_general(
        example_grads,
        own_rows,
        contract_last,
        precision=lax.Precision.HIGHEST,
        preferred_element_type=jnp.float32,
    )
    owned = (owner == lax.axis_index("bank")).astype(jnp.float32)[:, None]
    scores = lax.psum(partial_value * owned, ("tensor", "bank"))
    return scores


def params(cid, **more):
    return pltpu.CompilerParams(
        collective_id=cid, has_side_effects=True, vmem_limit_bytes=LIMIT, **more
    )


def greet(devices):
    barrier = pltpu.get_barrier_semaphore()
    for device in devices:
        pl.semaphore_signal(barrier, inc=1, device_id=device, device_id_type=MESH)
    pl.semaphore_wait(barrier, len(devices))


def layer_kernel(
    nz,
    half,
    tiles,
    tile,
    pick,
    grad,
    x_in,
    proj_in,
    proj_ff,
    weight,
    gate,
    up,
    part,
    wide,
    narrow,
    buf,
    packed,
    held,
    gate_in,
    up_in,
    act,
    rate,
    mine,
    sent,
    got,
    own_sem,
    fwd_sem,
    recv_sem,
    held_sem,
    gate_sem,
    up_sem,
    send_sem,
    got_sem,
):
    z, c = lax.axis_index("tensor"), lax.axis_index("pipe")
    other = 1 - c
    dest, place = z // half, z % half
    rank = proj_in.shape[0]
    width = packed.shape[1]
    rows = packed.shape[0] // PIECES
    part_rows = packed.shape[0] // 2
    events = 2 * PIECES
    barrier = pltpu.get_barrier_semaphore()
    pl.semaphore_signal(barrier, inc=1, device_id={"pipe": other}, device_id_type=MESH)
    for step in (-1, 1):

        @pl.when((z + step >= 0) & (z + step < nz))
        def _():
            for core in range(2):
                pl.semaphore_signal(
                    barrier,
                    inc=1,
                    device_id={"tensor": z + step, "pipe": core},
                    device_id_type=MESH,
                )

    def columns(t):
        return pl.ds(pl.multiple_of(t * tile, tile), tile)

    def hold(t):
        return pltpu.make_async_copy(weight.at[columns(t)], held.at[t], held_sem.at[t])

    def fetch(t, do):
        slot = t % 2
        do(pltpu.make_async_copy(gate.at[:, columns(t)], gate_in.at[slot], gate_sem.at[slot]))
        do(pltpu.make_async_copy(up.at[:, columns(t)], up_in.at[slot], up_sem.at[slot]))

    fetch(0, lambda d: d.start())
    fetch(1, lambda d: d.start())
    packed[...] = jnp.dot(pick[...], grad[...], preferred_element_type=jnp.float32).astype(
        jnp.bfloat16
    )
    pl.semaphore_wait(barrier, jnp.where((z > 0) & (z < nz - 1), 5, 3))

    def piece(q):
        return pl.ds(pl.multiple_of(q * rows, 16), rows)

    def own(way, q):
        return pltpu.make_async_remote_copy(
            src_ref=packed.at[piece(q)],
            dst_ref=buf.at[place, c, piece(q)],
            send_sem=own_sem.at[way, q],
            recv_sem=recv_sem.at[place, c, q],
            device_id={"tensor": z + (1, -1, 0)[way], "pipe": dest},
            device_id_type=MESH,
        )

    goes = (z < nz - 1, z > 0, dest != c)

    for q in range(PIECES):
        for way in range(3):

            @pl.when(goes[way])
            def _():
                own(way, q).start()

    @pl.loop(0, tiles)
    def _(t):
        hold(t).start()

    @pl.when(dest == c)
    def _():
        buf[place, c] = packed[...]

    packed_x = jnp.dot(pick[...], x_in[...], preferred_element_type=jnp.float32).astype(
        jnp.bfloat16
    )
    narrow[:, 0:rank] = lax.dot_general(
        packed_x, proj_in[...], LAST, preferred_element_type=jnp.float32
    )
    narrow[:, rank : 2 * rank] = lax.dot_general(
        packed[...], proj_in[...], LAST, preferred_element_type=jnp.float32
    )
    wide[...] = jnp.zeros_like(wide)

    def passed(j, k, q, step):
        return pltpu.make_async_remote_copy(
            src_ref=buf.at[j, k, piece(q)],
            dst_ref=buf.at[j, k, piece(q)],
            send_sem=fwd_sem.at[j, k, q],
            recv_sem=recv_sem.at[j, k, q],
            device_id={"tensor": z + step, "pipe": c},
            device_id_type=MESH,
        )

    def event(e):
        i, q, k = e // events, (e // 2) % PIECES, e % 2
        j = jnp.where(dest == c, i * place + (1 - i) * (1 - place), c * i + (1 - c) * (1 - i))
        return j, k, q, c * half + j

    def receive(e):
        j, k, q, source = event(e)

        @pl.when((source != z) | (k != c))
        def _():
            passed(j, k, q, 0).wait_recv()

        @pl.when((source < z) & (z < nz - 1))
        def _():
            passed(j, k, q, 1).start()

        @pl.when((source > z) & (z > 0))
        def _():
            passed(j, k, q, -1).start()

    @pl.loop(0, tiles)
    def _(t):
        slot = t % 2
        fetch(t, lambda d: d.wait())
        gate_val = jnp.dot(pick[...], gate_in[slot], preferred_element_type=jnp.float32)
        up_val = jnp.dot(pick[...], up_in[slot], preferred_element_type=jnp.float32)

        @pl.when(t + 2 < tiles)
        def _():
            fetch(t + 2, lambda d: d.start())

        sig = jax.nn.sigmoid(gate_val)
        silu = gate_val * sig
        act[t] = silu
        rate[t] = up_val * (sig * (1.0 + gate_val * (1.0 - sig)))
        wide[0] += lax.dot_general(
            (silu * up_val).astype(jnp.bfloat16),
            proj_ff[:, columns(t)],
            LAST,
            preferred_element_type=jnp.float32,
        )

        @pl.when((t % 2 == 1) & (t // 2 < events))
        def _():
            receive(t // 2)

    early = min(events, tiles // 2)
    middle = events + PIECES
    late = events * half - middle

    @pl.loop(early, middle)
    def _(e):
        receive(e)

    def copy(s):
        return pltpu.make_async_remote_copy(
            src_ref=sent.at[s],
            dst_ref=got.at[s],
            send_sem=send_sem.at[s],
            recv_sem=got_sem.at[s],
            device_id={"pipe": other},
            device_id_type=MESH,
        )

    def rows_of(s):
        return pl.ds(pl.multiple_of((s // tiles) * part_rows, 16), part_rows)

    def multiply(s):
        t, these = s % tiles, rows_of(s)
        total = None
        for j in range(half):
            left = jnp.concatenate([buf[j, other, these], buf[j, c, these]], axis=0)
            term = lax.dot_general(
                left,
                held[t, :, j * width : (j + 1) * width],
                LAST,
                preferred_element_type=jnp.float32,
            )
            total = term if total is None else total + term
        sent[s] = total[:part_rows].astype(jnp.bfloat16)
        copy(s).start()
        mine[s % (2 * LAG)] = total[part_rows:]

    def finish(s):
        t, these = s % tiles, rows_of(s)
        copy(s).wait_recv()
        hidden_grad = mine[s % (2 * LAG)] + got[s].astype(jnp.float32)
        table = proj_ff[:, columns(t)]
        for index, factor in ((1, act), (2, rate)):
            wide[index, these] += lax.dot_general(
                (hidden_grad * factor[t, these]).astype(jnp.bfloat16),
                table,
                LAST,
                preferred_element_type=jnp.float32,
            )

    @pl.loop(0, tiles)
    def _(s):
        hold(s).wait()
        multiply(s)

        @pl.when(s >= LAG)
        def _():
            finish(s - LAG)

        @pl.when((s % 4 == 3) & (s // 4 < late))
        def _():
            receive(middle + s // 4)

    for e in range(tiles // 4, late):
        receive(middle + e)

    @pl.loop(tiles, 2 * tiles)
    def _(s):
        multiply(s)
        finish(s - LAG)

    @pl.loop(2 * tiles - LAG, 2 * tiles)
    def _(s):
        finish(s)

    block = packed.shape[0] // nz
    for k in range(nz):
        low, mid, high = k * block, k * block + block // 2, (k + 1) * block
        part[k, 0:block, 0:rank] = wide[0, low:high]
        part[k, 0:block, rank:] = wide[1, low:high]
        part[k, block : 2 * block, 0:rank] = wide[2, low:high]
        part[k, block : 2 * block, rank:] = narrow[low:high, 0:rank]
        part[k, 2 * block :, 0:rank] = narrow[low:mid, rank:]
        part[k, 2 * block :, rank:] = narrow[mid:high, rank:]

    @pl.loop(0, 2 * tiles)
    def _(s):
        copy(s).wait_send()

    for q in range(PIECES):
        for way in range(3):

            @pl.when(goes[way])
            def _():
                own(way, q).wait_send()

    @pl.loop(0, events * half)
    def _(e):
        j, k, q, source = event(e)

        @pl.when(((source < z) & (z < nz - 1)) | ((source > z) & (z > 0)))
        def _():
            passed(j, k, q, 0).wait_send()


def tensor_sum_kernel(n, part, out, got, send_sem, recv_sem, send2, recv2):
    me = lax.axis_index("tensor")
    peers = [lax.rem(me + d, n) for d in range(1, n)]
    greet([{"tensor": peer} for peer in peers])

    def first(peer, slot):
        return pltpu.make_async_remote_copy(
            src_ref=part.at[peer],
            dst_ref=got.at[slot],
            send_sem=send_sem.at[peer],
            recv_sem=recv_sem.at[slot],
            device_id={"tensor": peer},
            device_id_type=MESH,
        )

    def second(peer, slot):
        return pltpu.make_async_remote_copy(
            src_ref=out.at[slot],
            dst_ref=out.at[slot],
            send_sem=send2.at[peer],
            recv_sem=recv2.at[slot],
            device_id={"tensor": peer},
            device_id_type=MESH,
        )

    for peer in peers:
        first(peer, me).start()
    got[me] = part[me]
    for peer in peers:
        first(peer, peer).wait_recv()
    total = got[0]
    for k in range(1, n):
        total = total + got[k]
    out[me] = total
    for peer in peers:
        second(peer, me).start()
    for peer in peers:
        second(peer, peer).wait_recv()
    for peer in peers:
        first(peer, me).wait_send()
        second(peer, me).wait_send()


def small_sum_kernel(axes, count_axes, *refs):
    if count_axes:
        part, count, out, counts, got, send_sem, recv_sem, csend, crecv = refs
    else:
        part, out, got, send_sem, recv_sem = refs

    def layout(names):
        sizes = [lax.axis_size(a) for a in names]
        me = lax.axis_index(names[0])
        for name, size in zip(names[1:], sizes[1:]):
            me = me * size + lax.axis_index(name)
        n = int(np.prod(sizes))
        peers = []
        for d in range(1, n):
            flat = lax.rem(me + d, n)
            rest, device = flat, {}
            for name, size in reversed(list(zip(names, sizes))):
                device[name] = lax.rem(rest, size)
                rest = rest // size
            peers.append((flat, device))
        return n, me, peers

    n, me, peers = layout(axes)

    def copy(flat, device, slot):
        return pltpu.make_async_remote_copy(
            src_ref=part,
            dst_ref=got.at[slot],
            send_sem=send_sem.at[flat],
            recv_sem=recv_sem.at[slot],
            device_id=device,
            device_id_type=MESH,
        )

    if count_axes:
        cn, cme, cpeers = layout(count_axes)

        def ccopy(flat, device, slot):
            return pltpu.make_async_remote_copy(
                src_ref=count,
                dst_ref=counts.at[slot],
                send_sem=csend.at[flat],
                recv_sem=crecv.at[slot],
                device_id=device,
                device_id_type=MESH,
            )

        greet([device for _, device in cpeers])
    else:
        greet([device for _, device in peers])
    for flat, device in peers:
        copy(flat, device, me).start()
    if count_axes:
        for flat, device in cpeers:
            ccopy(flat, device, cme).start()
        counts[cme] = count[...]
    got[me] = part[...]
    for flat, device in peers:
        copy(flat, device, flat).wait_recv()
    total = got[0]
    for k in range(1, n):
        total = total + got[k]
    out[...] = total
    for flat, device in peers:
        copy(flat, device, me).wait_send()
    if count_axes:
        for flat, device in cpeers:
            ccopy(flat, device, flat).wait_recv()
        for flat, device in cpeers:
            ccopy(flat, device, cme).wait_send()


def packed_body(
    x_in,
    grad_out,
    gate_pre,
    up_pre,
    w_down,
    proj_in,
    proj_ff,
    resp_mask,
    doc_lengths,
    owner,
    bank_grads,
):
    nz, npipe = lax.axis_size("tensor"), lax.axis_size("pipe")
    half = nz // npipe
    tokens, width = grad_out.shape
    hidden_units = gate_pre.shape[1]
    rank = proj_in.shape[1]
    tile = 256
    tiles = hidden_units // tile
    f32, b16 = jnp.float32, jnp.bfloat16
    dma = pltpu.SemaphoreType.DMA

    order = jnp.cumsum(resp_mask) - 1
    taken = jnp.sum(resp_mask)
    pick = ((order[None, :] == jnp.arange(CAP)[:, None]) & (resp_mask[None, :] > 0)).astype(b16)
    offset = lax.axis_index(("bank", "pipe")) * tokens
    positions = offset + jnp.arange(tokens, dtype=jnp.int32)
    doc_ends = jnp.cumsum(doc_lengths)
    starts = doc_ends - doc_lengths
    inside = (positions[:, None] >= starts[None, :]) & (positions[:, None] < doc_ends[None, :])
    member = jnp.dot(pick, inside.astype(b16), preferred_element_type=f32)
    nex = doc_lengths.shape[0]

    any_place = pl.BlockSpec(memory_space=pl.ANY)
    shape = (nz, 5 * CAP // (2 * nz), 2 * rank)
    partials = pl.pallas_call(
        functools.partial(layer_kernel, nz, half, tiles, tile),
        out_shape=jax.ShapeDtypeStruct(shape, f32),
        in_specs=[VMEM] * 5 + [any_place] * 3,
        out_specs=VMEM,
        scratch_shapes=[
            pltpu.VMEM((3, CAP, rank), f32),
            pltpu.VMEM((CAP, 2 * rank), f32),
            pltpu.VMEM((half, npipe, CAP, width), b16),
            pltpu.VMEM((CAP, width), b16),
            pltpu.VMEM((tiles, tile, half * width), b16),
            pltpu.VMEM((2, tokens, tile), b16),
            pltpu.VMEM((2, tokens, tile), b16),
            pltpu.VMEM((tiles, CAP, tile), f32),
            pltpu.VMEM((tiles, CAP, tile), f32),
            pltpu.VMEM((2 * LAG, CAP // 2, tile), f32),
            pltpu.VMEM((2 * tiles, CAP // 2, tile), b16),
            pltpu.VMEM((2 * tiles, CAP // 2, tile), b16),
            dma((3, PIECES)),
            dma((half, npipe, PIECES)),
            dma((half, npipe, PIECES)),
            dma((tiles,)),
            dma((2,)),
            dma((2,)),
            dma((2 * tiles,)),
            dma((2 * tiles,)),
        ],
        compiler_params=params(0),
        name="layer",
    )(pick, grad_out, x_in, proj_in.T, proj_ff.T, w_down, gate_pre, up_pre)

    projected = pl.pallas_call(
        functools.partial(tensor_sum_kernel, nz),
        out_shape=jax.ShapeDtypeStruct(shape, f32),
        in_specs=[VMEM],
        out_specs=VMEM,
        scratch_shapes=[pltpu.VMEM(shape, f32)] + [dma((nz,))] * 4,
        compiler_params=params(2),
        name="tensor_sum",
    )(partials)

    block = CAP // nz
    a_down = projected[:, :block, :rank].reshape(CAP, rank)
    b_up = projected[:, :block, rank:]
    b_gate = projected[:, block : 2 * block, :rank]
    b_wide = jnp.concatenate([b_up, b_gate], axis=2).reshape(CAP, 2 * rank)
    a_in = projected[:, block : 2 * block, rank:].reshape(CAP, rank)
    b_down = jnp.concatenate(
        [projected[:, 2 * block :, :rank], projected[:, 2 * block :, rank:]], axis=1
    ).reshape(CAP, rank)

    def grads(left, right):
        masked = (member[:, :, None] * left[:, None, :]).reshape(CAP, nex * rank)
        return lax.dot_general(
            masked,
            right,
            (((0,), (0,)), ((), ())),
            precision=lax.Precision.HIGHEST,
            preferred_element_type=f32,
        ).reshape(nex, rank, right.shape[1])

    first = grads(a_down, b_down)
    rest = grads(a_in, b_wide)
    whole = jnp.stack([first, rest[..., :rank], rest[..., rank:]], axis=1).reshape(nex, -1)
    kron_part = bank_grads.shape[2]
    mine = lax.dynamic_slice_in_dim(
        whole, lax.axis_index("tensor") * kron_part, kron_part, axis=1
    )

    def small_sum(part, axes, cid, count=None, count_axes=None):
        n = int(np.prod([lax.axis_size(a) for a in axes]))
        outs = [jax.ShapeDtypeStruct(part.shape, f32)]
        scratch = [pltpu.VMEM((n,) + part.shape, f32), dma((n,)), dma((n,))]
        operands = [part]
        if count_axes:
            cn = int(np.prod([lax.axis_size(a) for a in count_axes]))
            outs.append(jax.ShapeDtypeStruct((cn,) + count.shape, f32))
            scratch += [dma((cn,)), dma((cn,))]
            operands.append(count)
        return pl.pallas_call(
            functools.partial(small_sum_kernel, axes, count_axes),
            out_shape=tuple(outs),
            in_specs=[VMEM] * len(operands),
            out_specs=(VMEM,) * len(outs),
            scratch_shapes=scratch,
            compiler_params=params(cid),
            name="small_sum",
        )(*operands)

    example_grads, counts = small_sum(
        mine,
        ("bank", "pipe"),
        3,
        jnp.full((8, 128), taken, f32),
        ("groups", "bank", "pipe"),
    )
    partial_value = lax.dot_general(
        example_grads,
        bank_grads[0].astype(f32),
        LAST,
        precision=lax.Precision.HIGHEST,
        preferred_element_type=f32,
    )
    owned = (owner == lax.axis_index("bank")).astype(f32)[:, None]
    (scores,) = small_sum(partial_value * owned, ("tensor", "bank"), 4)
    return lax.cond(
        jnp.max(counts) > CAP,
        lambda: body(
            x_in,
            grad_out,
            gate_pre,
            up_pre,
            w_down,
            proj_in,
            proj_ff,
            resp_mask,
            doc_lengths,
            owner,
            bank_grads,
        ),
        lambda: scores,
    )


def choose(*args):
    nz = lax.axis_size("tensor")
    fits = (
        lax.axis_size("pipe") == 2
        and nz == 4
        and args[0].shape[0] >= CAP
        and CAP % (16 * nz) == 0
        and args[0].shape[1] % 128 == 0
        and args[2].shape[1] % 256 == 0
        and args[5].shape[1] == 64
    )
    return packed_body(*args) if fits else body(*args)


def solution(mesh):
    return jax.shard_map(
        choose,
        mesh=mesh,
        in_specs=(
            P(("groups", "bank", "pipe"), "tensor"),
            P(("groups", "bank", "pipe"), "tensor"),
            P(("groups", "bank", "pipe"), "tensor"),
            P(("groups", "bank", "pipe"), "tensor"),
            P("tensor", "pipe"),
            P("tensor", None),
            P("tensor", None),
            P(("groups", "bank", "pipe")),
            P("groups"),
            P("groups"),
            P("bank", "pipe", "tensor"),
        ),
        out_specs=P("groups", "pipe"),
        check_vma=False,
    )
```

```python
import functools
import jax
import jax.numpy as jnp
import numpy as np
from jax import lax
from jax.sharding import PartitionSpec as P
from jax.experimental import pallas as pl
from jax.experimental.pallas import tpu as pltpu

MESH = pl.DeviceIdType.MESH
VMEM = pl.BlockSpec(memory_space=pltpu.VMEM)
CAP = 320
PIECES = 4
LAG = 4
LIMIT = 60 * 1024 * 1024
LAST = (((1,), (1,)), ((), ()))


def body(
    x_in,
    grad_out,
    gate_pre,
    up_pre,
    w_down,
    proj_in,
    proj_ff,
    resp_mask,
    doc_lengths,
    owner,
    bank_grads,
):
    rows_here = x_in.shape[0]
    proj_rank = proj_in.shape[1]
    contract_last = (((1,), (1,)), ((), ()))
    full_rows = lax.all_gather(grad_out, "tensor", axis=1, tiled=True)
    paired = lax.all_to_all(full_rows, "pipe", split_axis=1, concat_axis=0, tiled=True)
    hidden_grad = lax.psum_scatter(
        lax.dot_general(paired, w_down, contract_last, preferred_element_type=jnp.float32),
        "pipe",
        scatter_dimension=0,
        tiled=True,
    )
    gate_val = gate_pre.astype(jnp.float32)
    up_val = up_pre.astype(jnp.float32)
    sigmoid_gate = jax.nn.sigmoid(gate_val)
    activated = gate_val * sigmoid_gate
    slope = sigmoid_gate * (1.0 + gate_val * (1.0 - sigmoid_gate))
    hidden = (activated * up_val).astype(jnp.bfloat16)
    up_grad = (hidden_grad * activated).astype(jnp.bfloat16)
    gate_grad = (hidden_grad * up_val * slope).astype(jnp.bfloat16)
    wide_side = jnp.stack([hidden, up_grad, gate_grad])
    wide_proj = jnp.einsum("stf,fr->srt", wide_side, proj_ff, preferred_element_type=jnp.float32)
    narrow_side = jnp.stack([x_in, grad_out])
    narrow_proj = jnp.einsum(
        "std,dr->srt", narrow_side, proj_in, preferred_element_type=jnp.float32
    )
    partials = jnp.concatenate([wide_proj, narrow_proj], axis=0)
    projected = lax.psum(partials, "tensor")
    stacked = projected.reshape(5 * proj_rank, rows_here)
    kron_part = bank_grads.shape[2]
    square = proj_rank * proj_rank
    module_ids = np.repeat(np.arange(3), square)
    inner_ids = np.arange(3 * square) % square
    left_table = np.array([0, 3, 3])[module_ids] * proj_rank + inner_ids // proj_rank
    right_table = np.array([4, 1, 2])[module_ids] * proj_rank + inner_ids % proj_rank
    first_entry = lax.axis_index("tensor") * kron_part
    left_ids = lax.dynamic_slice_in_dim(jnp.asarray(left_table, jnp.int32), first_entry, kron_part)
    right_ids = lax.dynamic_slice_in_dim(
        jnp.asarray(right_table, jnp.int32), first_entry, kron_part
    )
    products = jnp.take(stacked, left_ids, axis=0) * jnp.take(stacked, right_ids, axis=0)
    offset = lax.axis_index(("bank", "pipe")) * rows_here
    positions = offset + jnp.arange(rows_here, dtype=jnp.int32)
    doc_ends = jnp.cumsum(doc_lengths)
    starts = doc_ends - doc_lengths
    inside = (positions[:, None] >= starts[None, :]) & (positions[:, None] < doc_ends[None, :])
    member = inside.astype(jnp.float32) * resp_mask.astype(jnp.float32)[:, None]
    grad_part = lax.dot_general(
        member,
        products,
        (((0,), (1,)), ((), ())),
        precision=lax.Precision.HIGHEST,
        preferred_element_type=jnp.float32,
    )
    example_grads = lax.psum(grad_part, ("bank", "pipe"))
    own_rows = bank_grads[0].astype(jnp.float32)
    partial_value = lax.dot_general(
        example_grads,
        own_rows,
        contract_last,
        precision=lax.Precision.HIGHEST,
        preferred_element_type=jnp.float32,
    )
    owned = (owner == lax.axis_index("bank")).astype(jnp.float32)[:, None]
    scores = lax.psum(partial_value * owned, ("tensor", "bank"))
    return scores


def params(cid, **more):
    return pltpu.CompilerParams(
        collective_id=cid, has_side_effects=True, vmem_limit_bytes=LIMIT, **more
    )


def greet(devices):
    barrier = pltpu.get_barrier_semaphore()
    for device in devices:
        pl.semaphore_signal(barrier, inc=1, device_id=device, device_id_type=MESH)
    pl.semaphore_wait(barrier, len(devices))


def layer_kernel(
    nz,
    half,
    tiles,
    tile,
    pick,
    grad,
    x_in,
    proj_in,
    proj_ff,
    weight,
    gate,
    up,
    part,
    wide,
    narrow,
    buf,
    packed,
    held,
    gate_in,
    up_in,
    act,
    rate,
    mine,
    sent,
    got,
    own_sem,
    fwd_sem,
    recv_sem,
    held_sem,
    gate_sem,
    up_sem,
    send_sem,
    got_sem,
):
    z, c = lax.axis_index("tensor"), lax.axis_index("pipe")
    other = 1 - c
    dest, place = z // half, z % half
    rank = proj_in.shape[0]
    width = packed.shape[1]
    rows = packed.shape[0] // PIECES
    part_rows = packed.shape[0] // 2
    events = 2 * PIECES
    barrier = pltpu.get_barrier_semaphore()
    pl.semaphore_signal(barrier, inc=1, device_id={"pipe": other}, device_id_type=MESH)
    for step in (-1, 1):

        @pl.when((z + step >= 0) & (z + step < nz))
        def _():
            for core in range(2):
                pl.semaphore_signal(
                    barrier,
                    inc=1,
                    device_id={"tensor": z + step, "pipe": core},
                    device_id_type=MESH,
                )

    def columns(t):
        return pl.ds(pl.multiple_of(t * tile, tile), tile)

    def hold(t):
        return pltpu.make_async_copy(weight.at[columns(t)], held.at[t], held_sem.at[t])

    def fetch(t, do):
        slot = t % 2
        do(pltpu.make_async_copy(gate.at[:, columns(t)], gate_in.at[slot], gate_sem.at[slot]))
        do(pltpu.make_async_copy(up.at[:, columns(t)], up_in.at[slot], up_sem.at[slot]))

    fetch(0, lambda d: d.start())
    fetch(1, lambda d: d.start())
    packed[...] = jnp.dot(pick[...], grad[...], preferred_element_type=jnp.float32).astype(
        jnp.bfloat16
    )
    pl.semaphore_wait(barrier, jnp.where((z > 0) & (z < nz - 1), 5, 3))

    def piece(q):
        return pl.ds(pl.multiple_of(q * rows, 16), rows)

    def own(way, q):
        return pltpu.make_async_remote_copy(
            src_ref=packed.at[piece(q)],
            dst_ref=buf.at[place, c, piece(q)],
            send_sem=own_sem.at[way, q],
            recv_sem=recv_sem.at[place, c, q],
            device_id={"tensor": z + (1, -1, 0)[way], "pipe": dest},
            device_id_type=MESH,
        )

    goes = (z < nz - 1, z > 0, dest != c)

    for q in range(PIECES):
        for way in range(3):

            @pl.when(goes[way])
            def _():
                own(way, q).start()

    @pl.loop(0, tiles)
    def _(t):
        hold(t).start()

    @pl.when(dest == c)
    def _():
        buf[place, c] = packed[...]

    packed_x = jnp.dot(pick[...], x_in[...], preferred_element_type=jnp.float32).astype(
        jnp.bfloat16
    )
    narrow[:, 0:rank] = lax.dot_general(
        packed_x, proj_in[...], LAST, preferred_element_type=jnp.float32
    )
    narrow[:, rank : 2 * rank] = lax.dot_general(
        packed[...], proj_in[...], LAST, preferred_element_type=jnp.float32
    )
    wide[...] = jnp.zeros_like(wide)

    def passed(j, k, q, step):
        return pltpu.make_async_remote_copy(
            src_ref=buf.at[j, k, piece(q)],
            dst_ref=buf.at[j, k, piece(q)],
            send_sem=fwd_sem.at[j, k, q],
            recv_sem=recv_sem.at[j, k, q],
            device_id={"tensor": z + step, "pipe": c},
            device_id_type=MESH,
        )

    def event(e):
        i, q, k = (e // 4) % 2, 2 * (e // 8) + (e // 2) % 2, e % 2
        j = jnp.where(dest == c, i * place + (1 - i) * (1 - place), c * i + (1 - c) * (1 - i))
        return j, k, q, c * half + j

    def receive(e):
        j, k, q, source = event(e)

        @pl.when((source != z) | (k != c))
        def _():
            passed(j, k, q, 0).wait_recv()

        @pl.when((source < z) & (z < nz - 1))
        def _():
            passed(j, k, q, 1).start()

        @pl.when((source > z) & (z > 0))
        def _():
            passed(j, k, q, -1).start()

    @pl.loop(0, tiles)
    def _(t):
        slot = t % 2
        fetch(t, lambda d: d.wait())
        gate_val = jnp.dot(pick[...], gate_in[slot], preferred_element_type=jnp.float32)
        up_val = jnp.dot(pick[...], up_in[slot], preferred_element_type=jnp.float32)

        @pl.when(t + 2 < tiles)
        def _():
            fetch(t + 2, lambda d: d.start())

        sig = jax.nn.sigmoid(gate_val)
        silu = gate_val * sig
        act[t] = silu
        rate[t] = up_val * (sig * (1.0 + gate_val * (1.0 - sig)))
        wide[0] += lax.dot_general(
            (silu * up_val).astype(jnp.bfloat16),
            proj_ff[:, columns(t)],
            LAST,
            preferred_element_type=jnp.float32,
        )

        @pl.when((t % 2 == 1) & (t // 2 < events))
        def _():
            receive(t // 2)

    early = min(events, tiles // 2)
    middle = events
    late = events * half - middle

    @pl.loop(early, middle)
    def _(e):
        receive(e)

    def copy(s):
        return pltpu.make_async_remote_copy(
            src_ref=sent.at[s],
            dst_ref=got.at[s],
            send_sem=send_sem.at[s],
            recv_sem=got_sem.at[s],
            device_id={"pipe": other},
            device_id_type=MESH,
        )

    def rows_of(s):
        return pl.ds(pl.multiple_of((s // tiles) * part_rows, 16), part_rows)

    def multiply(s):
        t, these = s % tiles, rows_of(s)
        total = None
        for j in range(half):
            left = jnp.concatenate([buf[j, other, these], buf[j, c, these]], axis=0)
            term = lax.dot_general(
                left,
                held[t, :, j * width : (j + 1) * width],
                LAST,
                preferred_element_type=jnp.float32,
            )
            total = term if total is None else total + term
        sent[s] = total[:part_rows].astype(jnp.bfloat16)
        copy(s).start()
        mine[s % (2 * LAG)] = total[part_rows:]

    def finish(s):
        t, these = s % tiles, rows_of(s)
        copy(s).wait_recv()
        hidden_grad = mine[s % (2 * LAG)] + got[s].astype(jnp.float32)
        table = proj_ff[:, columns(t)]
        for index, factor in ((1, act), (2, rate)):
            wide[index, these] += lax.dot_general(
                (hidden_grad * factor[t, these]).astype(jnp.bfloat16),
                table,
                LAST,
                preferred_element_type=jnp.float32,
            )

    @pl.loop(0, tiles)
    def _(s):
        hold(s).wait()
        multiply(s)

        @pl.when(s >= LAG)
        def _():
            finish(s - LAG)

        @pl.when((s % 2 == 1) & (s // 2 < late))
        def _():
            receive(middle + s // 2)

    for e in range(tiles // 2, late):
        receive(middle + e)

    @pl.loop(tiles, 2 * tiles)
    def _(s):
        multiply(s)
        finish(s - LAG)

    @pl.loop(2 * tiles - LAG, 2 * tiles)
    def _(s):
        finish(s)

    block = packed.shape[0] // nz
    for k in range(nz):
        low, mid, high = k * block, k * block + block // 2, (k + 1) * block
        part[k, 0:block, 0:rank] = wide[0, low:high]
        part[k, 0:block, rank:] = wide[1, low:high]
        part[k, block : 2 * block, 0:rank] = wide[2, low:high]
        part[k, block : 2 * block, rank:] = narrow[low:high, 0:rank]
        part[k, 2 * block :, 0:rank] = narrow[low:mid, rank:]
        part[k, 2 * block :, rank:] = narrow[mid:high, rank:]

    @pl.loop(0, 2 * tiles)
    def _(s):
        copy(s).wait_send()

    for q in range(PIECES):
        for way in range(3):

            @pl.when(goes[way])
            def _():
                own(way, q).wait_send()

    @pl.loop(0, events * half)
    def _(e):
        j, k, q, source = event(e)

        @pl.when(((source < z) & (z < nz - 1)) | ((source > z) & (z > 0)))
        def _():
            passed(j, k, q, 0).wait_send()


def tensor_sum_kernel(n, part, out, got, send_sem, recv_sem, send2, recv2):
    me = lax.axis_index("tensor")
    peers = [lax.rem(me + d, n) for d in range(1, n)]
    greet([{"tensor": peer} for peer in peers])

    def first(peer, slot):
        return pltpu.make_async_remote_copy(
            src_ref=part.at[peer],
            dst_ref=got.at[slot],
            send_sem=send_sem.at[peer],
            recv_sem=recv_sem.at[slot],
            device_id={"tensor": peer},
            device_id_type=MESH,
        )

    def second(peer, slot):
        return pltpu.make_async_remote_copy(
            src_ref=out.at[slot],
            dst_ref=out.at[slot],
            send_sem=send2.at[peer],
            recv_sem=recv2.at[slot],
            device_id={"tensor": peer},
            device_id_type=MESH,
        )

    for peer in peers:
        first(peer, me).start()
    got[me] = part[me]
    for peer in peers:
        first(peer, peer).wait_recv()
    total = got[0]
    for k in range(1, n):
        total = total + got[k]
    out[me] = total
    for peer in peers:
        second(peer, me).start()
    for peer in peers:
        second(peer, peer).wait_recv()
    for peer in peers:
        first(peer, me).wait_send()
        second(peer, me).wait_send()


def small_sum_kernel(axes, count_axes, *refs):
    if count_axes:
        part, count, out, counts, got, send_sem, recv_sem, csend, crecv = refs
    else:
        part, out, got, send_sem, recv_sem = refs

    def layout(names):
        sizes = [lax.axis_size(a) for a in names]
        me = lax.axis_index(names[0])
        for name, size in zip(names[1:], sizes[1:]):
            me = me * size + lax.axis_index(name)
        n = int(np.prod(sizes))
        peers = []
        for d in range(1, n):
            flat = lax.rem(me + d, n)
            rest, device = flat, {}
            for name, size in reversed(list(zip(names, sizes))):
                device[name] = lax.rem(rest, size)
                rest = rest // size
            peers.append((flat, device))
        return n, me, peers

    n, me, peers = layout(axes)

    def copy(flat, device, slot):
        return pltpu.make_async_remote_copy(
            src_ref=part,
            dst_ref=got.at[slot],
            send_sem=send_sem.at[flat],
            recv_sem=recv_sem.at[slot],
            device_id=device,
            device_id_type=MESH,
        )

    if count_axes:
        cn, cme, cpeers = layout(count_axes)

        def ccopy(flat, device, slot):
            return pltpu.make_async_remote_copy(
                src_ref=count,
                dst_ref=counts.at[slot],
                send_sem=csend.at[flat],
                recv_sem=crecv.at[slot],
                device_id=device,
                device_id_type=MESH,
            )

        greet([device for _, device in cpeers])
    else:
        greet([device for _, device in peers])
    for flat, device in peers:
        copy(flat, device, me).start()
    if count_axes:
        for flat, device in cpeers:
            ccopy(flat, device, cme).start()
        counts[cme] = count[...]
    got[me] = part[...]
    for flat, device in peers:
        copy(flat, device, flat).wait_recv()
    total = got[0]
    for k in range(1, n):
        total = total + got[k]
    out[...] = total
    for flat, device in peers:
        copy(flat, device, me).wait_send()
    if count_axes:
        for flat, device in cpeers:
            ccopy(flat, device, flat).wait_recv()
        for flat, device in cpeers:
            ccopy(flat, device, cme).wait_send()


def packed_body(
    x_in,
    grad_out,
    gate_pre,
    up_pre,
    w_down,
    proj_in,
    proj_ff,
    resp_mask,
    doc_lengths,
    owner,
    bank_grads,
):
    nz, npipe = lax.axis_size("tensor"), lax.axis_size("pipe")
    half = nz // npipe
    tokens, width = grad_out.shape
    hidden_units = gate_pre.shape[1]
    rank = proj_in.shape[1]
    tile = 256
    tiles = hidden_units // tile
    f32, b16 = jnp.float32, jnp.bfloat16
    dma = pltpu.SemaphoreType.DMA

    order = jnp.cumsum(resp_mask) - 1
    taken = jnp.sum(resp_mask)
    pick = ((order[None, :] == jnp.arange(CAP)[:, None]) & (resp_mask[None, :] > 0)).astype(b16)
    offset = lax.axis_index(("bank", "pipe")) * tokens
    positions = offset + jnp.arange(tokens, dtype=jnp.int32)
    doc_ends = jnp.cumsum(doc_lengths)
    starts = doc_ends - doc_lengths
    inside = (positions[:, None] >= starts[None, :]) & (positions[:, None] < doc_ends[None, :])
    member = jnp.dot(pick, inside.astype(b16), preferred_element_type=f32)
    nex = doc_lengths.shape[0]

    any_place = pl.BlockSpec(memory_space=pl.ANY)
    shape = (nz, 5 * CAP // (2 * nz), 2 * rank)
    partials = pl.pallas_call(
        functools.partial(layer_kernel, nz, half, tiles, tile),
        out_shape=jax.ShapeDtypeStruct(shape, f32),
        in_specs=[VMEM] * 5 + [any_place] * 3,
        out_specs=VMEM,
        scratch_shapes=[
            pltpu.VMEM((3, CAP, rank), f32),
            pltpu.VMEM((CAP, 2 * rank), f32),
            pltpu.VMEM((half, npipe, CAP, width), b16),
            pltpu.VMEM((CAP, width), b16),
            pltpu.VMEM((tiles, tile, half * width), b16),
            pltpu.VMEM((2, tokens, tile), b16),
            pltpu.VMEM((2, tokens, tile), b16),
            pltpu.VMEM((tiles, CAP, tile), f32),
            pltpu.VMEM((tiles, CAP, tile), f32),
            pltpu.VMEM((2 * LAG, CAP // 2, tile), f32),
            pltpu.VMEM((2 * tiles, CAP // 2, tile), b16),
            pltpu.VMEM((2 * tiles, CAP // 2, tile), b16),
            dma((3, PIECES)),
            dma((half, npipe, PIECES)),
            dma((half, npipe, PIECES)),
            dma((tiles,)),
            dma((2,)),
            dma((2,)),
            dma((2 * tiles,)),
            dma((2 * tiles,)),
        ],
        compiler_params=params(0),
        name="layer",
    )(pick, grad_out, x_in, proj_in.T, proj_ff.T, w_down, gate_pre, up_pre)

    projected = pl.pallas_call(
        functools.partial(tensor_sum_kernel, nz),
        out_shape=jax.ShapeDtypeStruct(shape, f32),
        in_specs=[VMEM],
        out_specs=VMEM,
        scratch_shapes=[pltpu.VMEM(shape, f32)] + [dma((nz,))] * 4,
        compiler_params=params(2),
        name="tensor_sum",
    )(partials)

    block = CAP // nz
    a_down = projected[:, :block, :rank].reshape(CAP, rank)
    b_up = projected[:, :block, rank:]
    b_gate = projected[:, block : 2 * block, :rank]
    b_wide = jnp.concatenate([b_up, b_gate], axis=2).reshape(CAP, 2 * rank)
    a_in = projected[:, block : 2 * block, rank:].reshape(CAP, rank)
    b_down = jnp.concatenate(
        [projected[:, 2 * block :, :rank], projected[:, 2 * block :, rank:]], axis=1
    ).reshape(CAP, rank)

    def grads(left, right):
        masked = (member[:, :, None] * left[:, None, :]).reshape(CAP, nex * rank)
        return lax.dot_general(
            masked,
            right,
            (((0,), (0,)), ((), ())),
            precision=lax.Precision.HIGHEST,
            preferred_element_type=f32,
        ).reshape(nex, rank, right.shape[1])

    first = grads(a_down, b_down)
    rest = grads(a_in, b_wide)
    whole = jnp.stack([first, rest[..., :rank], rest[..., rank:]], axis=1).reshape(nex, -1)
    kron_part = bank_grads.shape[2]
    mine = lax.dynamic_slice_in_dim(
        whole, lax.axis_index("tensor") * kron_part, kron_part, axis=1
    )

    def small_sum(part, axes, cid, count=None, count_axes=None):
        n = int(np.prod([lax.axis_size(a) for a in axes]))
        outs = [jax.ShapeDtypeStruct(part.shape, f32)]
        scratch = [pltpu.VMEM((n,) + part.shape, f32), dma((n,)), dma((n,))]
        operands = [part]
        if count_axes:
            cn = int(np.prod([lax.axis_size(a) for a in count_axes]))
            outs.append(jax.ShapeDtypeStruct((cn,) + count.shape, f32))
            scratch += [dma((cn,)), dma((cn,))]
            operands.append(count)
        return pl.pallas_call(
            functools.partial(small_sum_kernel, axes, count_axes),
            out_shape=tuple(outs),
            in_specs=[VMEM] * len(operands),
            out_specs=(VMEM,) * len(outs),
            scratch_shapes=scratch,
            compiler_params=params(cid),
            name="small_sum",
        )(*operands)

    example_grads, counts = small_sum(
        mine,
        ("bank", "pipe"),
        3,
        jnp.full((8, 128), taken, f32),
        ("groups", "bank", "pipe"),
    )
    partial_value = lax.dot_general(
        example_grads,
        bank_grads[0].astype(f32),
        LAST,
        precision=lax.Precision.HIGHEST,
        preferred_element_type=f32,
    )
    owned = (owner == lax.axis_index("bank")).astype(f32)[:, None]
    (scores,) = small_sum(partial_value * owned, ("tensor", "bank"), 4)
    return lax.cond(
        jnp.max(counts) > CAP,
        lambda: body(
            x_in,
            grad_out,
            gate_pre,
            up_pre,
            w_down,
            proj_in,
            proj_ff,
            resp_mask,
            doc_lengths,
            owner,
            bank_grads,
        ),
        lambda: scores,
    )


def choose(*args):
    nz = lax.axis_size("tensor")
    fits = (
        lax.axis_size("pipe") == 2
        and nz == 4
        and args[0].shape[0] >= CAP
        and CAP % (16 * nz) == 0
        and args[0].shape[1] % 128 == 0
        and args[2].shape[1] % 256 == 0
        and args[5].shape[1] == 64
    )
    return packed_body(*args) if fits else body(*args)


def solution(mesh):
    return jax.shard_map(
        choose,
        mesh=mesh,
        in_specs=(
            P(("groups", "bank", "pipe"), "tensor"),
            P(("groups", "bank", "pipe"), "tensor"),
            P(("groups", "bank", "pipe"), "tensor"),
            P(("groups", "bank", "pipe"), "tensor"),
            P("tensor", "pipe"),
            P("tensor", None),
            P("tensor", None),
            P(("groups", "bank", "pipe")),
            P("groups"),
            P("groups"),
            P("bank", "pipe", "tensor"),
        ),
        out_specs=P("groups", "pipe"),
        check_vma=False,
    )
```
